32 devices in a mesh: seq: 8 (over z, x), book: 4 (over y, core).
Axes of the slice: x: 2, y: 2, z: 4, core: 2. Of those that a mesh axis runs over, the one named last changes fastest.
Arguments:
- features: bfloat16 [4, 1024, 512], P('book', 'seq'), may hold values from -6 to 6
- lengths: int32 [4, 8], P('book'), may hold values from 1 to 256, 1024 in all within a row
- owner: int32 [4, 1024, 1], P('book', 'seq'), may hold values from 0 to 7; in each aligned block of 128 rows (0 to 127, 128 to 255, ..., all dimensions but the last counted through in order) at most 17 rows name the same one
- w_enc: bfloat16 [3, 512, 256], replicated, may hold values from -0.15625 to 0.15625
- w_in: bfloat16 [256, 2048], P(None, ('seq', 'book')), may hold values from -0.375 to 0.375
- gain: float32 [2048], replicated, may hold values from 0.1 to 1.9
- cotangent: bfloat16 [4, 1088, 2048], P('book', 'seq'), may hold values from -6 to 6
Outputs:
- grad_features: bfloat16 [4, 1024, 512], P('book', 'seq')
- grad_w_enc: float32 [3, 512, 256], P(None, 'book')
- grad_w_in: float32 [256, 2048], P(None, ('seq', 'book'))
- grad_gain: float32 [2048], replicated
The draws below stay inside these ranges and needn't reach their ends.
Inputs may be any that keep to these rules, and one draw needn't show every extreme that they name: Of the 128 frames of one device's block no more than 17 have the same owner, and in some block exactly 17 do. The 8 lengths of a stream sum to 1024; the largest is 256.
All inputs are finite; a program needn't handle non-finite values.
Results may differ from the reference program's by a relative error of at most 0.0095.
Values may be sent and summed in bfloat16 or wider, within the bound.
No kernel may reach another device: no remote copies, remote signals or barrier semaphores. Data moves between devices by JAX's collectives and lax.ppermute only.
A program may use at most 64 MiB of HBM per device.

```python
import math
import jax
import jax.numpy as jnp
import numpy as np
from jax import lax

DM = 2048
C_IN = 512
LAT = 256
KW = 3
NB = 8
FR = 128
CAP = 17
TOTAL = 1024
SLOTS = 1088
N_SEQ = 8
N_BOOK = 4


def raised(result, stream_key, source, target, blocks, factor):
    owner, partner = [(jnp.arange(result.shape[dim]) // (result.shape[dim] // blocks)).reshape([-1 if axis == dim else 1 for axis in range(result.ndim)]) for dim in (source, target)]
    chosen = jax.random.permutation(stream_key, blocks)[partner]
    strong = (owner == chosen) | (owner == (partner + blocks // 2) % blocks)
    return jnp.where(strong, factor * result, result)


def level_of(rng, dims, split, low, high):
    def one(dim, shards_of):
        heights = jax.random.uniform(jax.random.fold_in(jax.random.fold_in(rng, 6), dim), (shards_of,), jnp.float32, low / len(split), high / len(split))
        return jnp.repeat(jnp.exp(heights), dims[dim] // shards_of).reshape((-1,) + (1,) * (len(dims) - dim - 1))

    loudness = one(*split[0])
    for cut in split[1:]:
        loudness = loudness * one(*cut)
    return loudness


def split_up(count, total, most, skew):
    loads = [(1 << 20) // math.isqrt(standing ** skew) + 1 for standing in range(2, count + 1)]
    rest, holding = total - most - (count - 1), [1] * (count - 1)
    while rest > 0:
        movable = [i for i in range(count - 1) if holding[i] < most]
        whole, left = sum([loads[i] for i in movable]), rest
        for i in movable:
            addition = min(most - holding[i], max(1, left * loads[i] // whole), rest)
            holding[i] = holding[i] + addition
            rest = rest - addition
    return np.array([most] + holding)


def uneven_parts(rng, count, total, limit, skew):
    if count == 2:
        one = jax.random.randint(rng, (), max(1, total - limit), min(limit, total - 1) + 1)
        return jnp.stack([one, total - one])
    tallies = jnp.asarray(split_up(count, total, limit, skew), jnp.int32)
    couples = (count - 1) // 2
    giver, sink = tallies[1:1 + 2 * couples:2], tallies[2:2 + 2 * couples:2]
    margin = jnp.minimum(giver - 1, limit - sink)
    passed = jax.random.randint(jax.random.fold_in(rng, 1), (couples,), 0, 1 << 20) % (margin + 1)
    tallies = tallies.at[1:1 + 2 * couples:2].set(giver - passed).at[2:2 + 2 * couples:2].set(sink + passed)
    return tallies[jax.random.permutation(jax.random.fold_in(rng, 2), count)]


def assign_block(rng, own, number, rows, count, top, reach, skew):
    order = jax.random.permutation(rng, count)
    crowded, ordinary = load_shares(count, rows * top, reach, skew, True), load_shares(count, rows * top, reach, skew, False)
    places = jnp.arange(count)

    def named(tallies, offset_by):
        used = int((tallies > 0).sum())
        fixed = max(1, used // 4)
        moved = fixed + (places - fixed + offset_by * (used - fixed)) % max(1, count - fixed)
        return jnp.zeros((count,), jnp.int32).at[order[jnp.where(places < fixed, places, moved)]].set(jnp.asarray(tallies, jnp.int32))

    tallies = jnp.where(number % 4 == 0, named(crowded, number // 4), named(ordinary, number - number // 4 - 1))
    mixed = jax.random.permutation(jax.random.fold_in(own, 3), count)
    source_of, sink = mixed[0:count // 2 * 2:2], mixed[1:count // 2 * 2:2]
    room = jnp.minimum(tallies[source_of] - 1, reach - tallies[sink]) // 2
    room = jnp.where((source_of == order[0]) | (sink == order[0]) | (tallies[sink] == 0), 0, jnp.maximum(room, 0))
    moved = jax.random.randint(jax.random.fold_in(own, 4), (count // 2,), 0, 1 << 20) % (room + 1)
    tallies = tallies.at[source_of].add(-moved).at[sink].add(moved)
    labels = jnp.searchsorted(jnp.cumsum(tallies), jnp.arange(rows * top), side="right").astype(jnp.int32)
    listing = labels.reshape(top, rows).T
    listing = listing[jax.random.permutation(jax.random.fold_in(own, 1), rows)]
    offset_by = jax.random.randint(jax.random.fold_in(own, 2), (rows, 1), 0, top)
    return jnp.take_along_axis(listing, (jnp.arange(top)[None, :] + offset_by) % top, axis=1)


def load_shares(count, total, bound, skew, full):
    portions = [(1 << 20) // math.isqrt(rank ** skew) + 1 for rank in range(1, count + 1)]
    largest = bound if full else min(bound, max(-(-total // count), total * portions[0] // sum(portions)))
    least = 1 if total - largest >= count - 1 else 0
    counts, rest = [largest] + [least] * (count - 1), total - largest - least * (count - 1)
    while rest > 0:
        movable = [i for i in range(1, count) if counts[i] < largest] or [i for i in range(1, count) if counts[i] < bound]
        whole, budget = sum([portions[i] for i in movable]), rest
        for i in movable:
            addition = min(bound - counts[i], max(1, budget * portions[i] // whole), rest)
            counts[i] = counts[i] + addition
            rest = rest - addition
    return np.array(counts)


def gaussian(own_key, extent, width, most, shards=(), kind=jnp.bfloat16):
    values = width * jax.random.normal(own_key, extent, jnp.float32)
    if shards:
        values = values * level_of(own_key, extent, shards, -0.22, 0.18)
    return jnp.clip(values, -most, most).astype(kind)


def noise_with(stream_key, shape, width, most, shards, heavy, kind=jnp.bfloat16):
    drawn = width * jax.random.normal(stream_key, shape, jnp.float32)
    if shards:
        drawn = drawn * level_of(stream_key, shape, shards, -0.22, 0.18)
    return jnp.clip(raised(drawn, jax.random.fold_in(stream_key, 3), *heavy), -most, most).astype(kind)


def setup_inputs(seed: int = 0) -> dict:
    arg_keys = jax.random.split(jax.random.key(seed), 8)
    features = gaussian(arg_keys[0], (N_BOOK, TOTAL, C_IN), 1.0, 6.0, ((0, 4), (1, 8)))
    lengths = jax.vmap(lambda own: uneven_parts(own, NB, TOTAL, TOTAL // 4, 2))(jax.random.split(arg_keys[1], N_BOOK)).reshape((N_BOOK, NB)).astype(jnp.int32)
    owner_keys = jax.random.split(jax.random.fold_in(arg_keys[2], 1), N_BOOK * TOTAL // FR)
    owner_turns = jax.random.permutation(jax.random.fold_in(arg_keys[2], 3), N_BOOK * TOTAL // FR)
    owner = jax.vmap(lambda own, number: assign_block(jax.random.fold_in(arg_keys[2], 2), own, number, FR, N_SEQ, 1, CAP, 2))(owner_keys, owner_turns).reshape((N_BOOK, TOTAL, 1))
    w_enc = gaussian(arg_keys[3], (KW, C_IN, LAT), (KW * C_IN) ** -0.5, 0.15625)
    w_in = gaussian(arg_keys[4], (LAT, DM), LAT ** -0.5, 0.375, ((1, 32),))
    gain = jnp.clip(1.0 + 0.18 * jax.random.normal(arg_keys[5], (DM,), jnp.float32), 0.1, 1.9)
    cotangent = noise_with(arg_keys[6], (N_BOOK, SLOTS, DM), 1.0, 6.0, ((0, 4), (1, 8)), (1, 2, 8, 2.0))
    return dict(features=features, lengths=lengths, owner=owner, w_enc=w_enc, w_in=w_in, gain=gain, cotangent=cotangent)


def book_starts(book_lengths, position):
    starts = jnp.cumsum(book_lengths) - book_lengths
    return lax.optimization_barrier(jnp.max(jnp.where(starts[None, :] <= position[:, None], starts[None, :], 0), axis=1))

def stream_grads(feature_rows, book_lengths, owner_rows, cotangent_rows, w_enc, w_full, gain):
    total_frames, channels = feature_rows.shape
    latent_width = w_enc.shape[2]
    frames = total_frames // N_SEQ
    capacity = max(2, frames // N_SEQ + 1)
    position = jnp.arange(total_frames, dtype=jnp.int32)
    start_of = book_starts(book_lengths, position)
    feats_wide = feature_rows.astype(jnp.float32)
    activated = jax.nn.elu(feats_wide).astype(jnp.bfloat16)
    tap_inputs = []
    tap_masks = []
    for offset in range(KW):
        shifted = jnp.concatenate([jnp.zeros((offset, channels), jnp.bfloat16), activated[:total_frames - offset]], axis=0)
        valid_tap = position - offset >= start_of
        tap_masks.append(valid_tap)
        tap_inputs.append(jnp.where(valid_tap[:, None], shifted, jnp.zeros_like(shifted)))
    stacked = jnp.concatenate(tap_inputs, axis=1)
    latent = jnp.dot(stacked, w_enc.reshape(KW * channels, latent_width), preferred_element_type=jnp.float32).astype(jnp.bfloat16)
    owner_rank = owner_rows[:, 0]
    one_hot = (owner_rank.reshape(N_SEQ, frames)[:, :, None] == jnp.arange(N_SEQ, dtype=jnp.int32)[None, None, :]).astype(jnp.int32)
    slot_rank = lax.optimization_barrier(jnp.sum((jnp.cumsum(one_hot, axis=1) - one_hot) * one_hot, axis=2)).reshape(total_frames)
    slot_index = (owner_rank * (N_SEQ * capacity) + position // frames * capacity + slot_rank).astype(jnp.int32)
    grad_out = cotangent_rows[slot_index].astype(jnp.float32)
    hidden = jnp.dot(latent, w_full, preferred_element_type=jnp.float32)
    inv_rms = lax.rsqrt(lax.optimization_barrier(jnp.mean(hidden * hidden, axis=1, keepdims=True)) + 1e-05)
    normed = hidden * inv_rms
    gain_term = grad_out * gain[None, :]
    hidden_grad = (inv_rms * (gain_term - normed * lax.optimization_barrier(jnp.mean(gain_term * normed, axis=1, keepdims=True)))).astype(jnp.bfloat16)
    latent_grad = jnp.dot(hidden_grad, w_full.T, preferred_element_type=jnp.float32).astype(jnp.bfloat16)
    w_in_grad = jnp.dot(latent.T, hidden_grad, preferred_element_type=jnp.float32)
    gain_grad = lax.optimization_barrier(jnp.sum(grad_out * normed, axis=0))
    activ_grad = jnp.zeros((total_frames, channels), jnp.float32)
    for offset in range(KW):
        masked = jnp.where(tap_masks[offset][:, None], latent_grad, jnp.zeros_like(latent_grad))
        moved = jnp.concatenate([masked[offset:], jnp.zeros((offset, latent_width), jnp.bfloat16)], axis=0)
        activ_grad = activ_grad + jnp.dot(moved, w_enc[offset].T, preferred_element_type=jnp.float32)
    kernel_grad = jnp.dot(stacked.T, latent_grad, preferred_element_type=jnp.float32).reshape(KW, channels, latent_width)
    slope = jnp.where(feats_wide > 0, 1.0, jnp.exp(feats_wide))
    feature_grad = (slope * activ_grad).astype(jnp.bfloat16)
    return (feature_grad, kernel_grad, w_in_grad, gain_grad)

def reference(features, lengths, owner, w_enc, w_in, gain, cotangent):

    def per_stream(stream_args):
        return stream_grads(stream_args[0], stream_args[1], stream_args[2], stream_args[3], w_enc, w_in, gain)
    feature_grad, kernel_grad, w_in_grad, gain_grad = lax.map(per_stream, (features, lengths, owner, cotangent))
    return (feature_grad, lax.optimization_barrier(jnp.sum(kernel_grad, axis=0)), lax.optimization_barrier(jnp.sum(w_in_grad, axis=0)), lax.optimization_barrier(jnp.sum(gain_grad, axis=0)))
```

```python
import functools

import jax
import jax.numpy as jnp
from jax import lax
from jax.experimental import pallas as pl
from jax.experimental.pallas import tpu as pltpu
from jax.sharding import PartitionSpec as P

F32 = jnp.float32
BF16 = jnp.bfloat16
VMEM = pl.BlockSpec(memory_space=pltpu.VMEM)
SMEM = pl.BlockSpec(memory_space=pltpu.SMEM)


def shifted(block, axis, distance):
    devices = range(lax.axis_size(axis))
    route = [(i - distance, i) for i in devices if i - distance in devices]
    return lax.ppermute(block, axis, route)


def book_mask(position, book_lengths, offset):
    starts = jnp.cumsum(book_lengths) - book_lengths
    start_of = jnp.max(jnp.where(starts[None, :] <= position[:, None], starts[None, :], 0), axis=1)
    return position - offset >= start_of


def per_device_gather(features, lengths, owner, w_enc, w_in, gain, cotangent):
    feature_rows = features[0]
    frames, channels = feature_rows.shape
    tap_count, _, latent_width = w_enc.shape
    seq_count = lax.axis_size("seq")
    book_count = lax.axis_size("book")
    capacity = max(2, frames // seq_count + 1)
    first_frame = lax.axis_index("seq") * frames
    position = first_frame + jnp.arange(frames + tap_count - 1, dtype=jnp.int32)
    tap_masks = [book_mask(position, lengths[0], offset) for offset in range(tap_count)]
    feats_wide = feature_rows.astype(jnp.float32)
    activated = jax.nn.elu(feats_wide).astype(jnp.bfloat16)
    left_edge = shifted(activated[frames - (tap_count - 1) :], "seq", 1)
    padded = jnp.concatenate([left_edge, activated], axis=0)
    tap_inputs = []
    for offset in range(tap_count):
        begin = tap_count - 1 - offset
        window = padded[begin : begin + frames]
        tap_inputs.append(
            jnp.where(tap_masks[offset][:frames, None], window, jnp.zeros_like(window))
        )
    stacked = jnp.concatenate(tap_inputs, axis=1)
    latent = jnp.dot(
        stacked,
        w_enc.reshape(tap_count * channels, latent_width),
        preferred_element_type=jnp.float32,
    ).astype(jnp.bfloat16)
    owner_rank = owner[0, :, 0]
    one_hot = (owner_rank[:, None] == jnp.arange(seq_count, dtype=jnp.int32)[None, :]).astype(
        jnp.int32
    )
    slot_rank = jnp.sum((jnp.cumsum(one_hot, axis=0) - one_hot) * one_hot, axis=1)
    slot_index = owner_rank * capacity + slot_rank
    placement = (
        slot_index[:, None] == jnp.arange(seq_count * capacity, dtype=jnp.int32)[None, :]
    ).astype(jnp.bfloat16)
    outgoing = lax.dot_general(
        placement, latent, (((0,), (0,)), ((), ())), preferred_element_type=jnp.float32
    ).astype(jnp.bfloat16)
    arrived = lax.all_to_all(
        outgoing.reshape(seq_count, capacity, latent_width),
        "seq",
        split_axis=0,
        concat_axis=0,
        tiled=True,
    )
    arrived = arrived.reshape(seq_count * capacity, latent_width)
    w_full = lax.all_gather(w_in, ("seq", "book"), axis=1, tiled=True)
    grad_out = cotangent[0].astype(jnp.float32)
    hidden = jnp.dot(arrived, w_full, preferred_element_type=jnp.float32)
    inv_rms = lax.rsqrt(jnp.mean(hidden * hidden, axis=1, keepdims=True) + 1e-05)
    normed = hidden * inv_rms
    gain_term = grad_out * gain[None, :]
    hidden_grad = (
        inv_rms * (gain_term - normed * jnp.mean(gain_term * normed, axis=1, keepdims=True))
    ).astype(jnp.bfloat16)
    latent_back = lax.dot_general(
        hidden_grad, w_full, (((1,), (1,)), ((), ())), preferred_element_type=jnp.float32
    ).astype(jnp.bfloat16)
    w_part = lax.dot_general(
        arrived, hidden_grad, (((0,), (0,)), ((), ())), preferred_element_type=jnp.float32
    )
    gain_part = jnp.sum(grad_out * normed, axis=0)
    returned = lax.all_to_all(
        latent_back.reshape(seq_count, capacity, latent_width),
        "seq",
        split_axis=0,
        concat_axis=0,
        tiled=True,
    )
    returned = returned.reshape(seq_count * capacity, latent_width)
    latent_grad = jnp.dot(placement, returned, preferred_element_type=jnp.float32).astype(
        jnp.bfloat16
    )
    right_edge = shifted(latent_grad[: tap_count - 1], "seq", -1)
    extended = jnp.concatenate([latent_grad, right_edge], axis=0)
    tap_grads = []
    for offset in range(tap_count):
        window = extended[offset : offset + frames]
        tap_grads.append(
            jnp.where(
                tap_masks[offset][offset : offset + frames, None], window, jnp.zeros_like(window)
            )
        )
    kernel_back = jnp.transpose(w_enc, (0, 2, 1)).reshape(tap_count * latent_width, channels)
    activ_grad = jnp.dot(
        jnp.concatenate(tap_grads, axis=1), kernel_back, preferred_element_type=jnp.float32
    )
    slope = jnp.where(feats_wide > 0, 1.0, jnp.exp(feats_wide))
    feature_grad = (slope * activ_grad).astype(jnp.bfloat16)
    kernel_part = lax.dot_general(
        stacked, latent_grad, (((0,), (0,)), ((), ())), preferred_element_type=jnp.float32
    )
    kernel_part = kernel_part.reshape(tap_count, channels, latent_width)
    kernel_total, gain_total = lax.psum((kernel_part, gain_part), ("seq", "book"))
    share_width = channels // book_count
    kernel_mine = lax.dynamic_slice_in_dim(
        kernel_total, lax.axis_index("book") * share_width, share_width, 1
    )
    columns = w_in.shape[1]
    split_grad = w_part.reshape(latent_width, seq_count, book_count * columns)
    split_grad = lax.psum_scatter(
        split_grad.astype(jnp.bfloat16), "book", scatter_dimension=2, tiled=True
    ).astype(jnp.float32)
    w_grad = lax.psum_scatter(split_grad, "seq", scatter_dimension=1, tiled=True).reshape(
        latent_width, columns
    )
    return (feature_grad[None], kernel_mine, w_grad, gain_total)


def round_up(value, unit):
    return -(-value // unit) * unit


def swap(block, axis, mask):
    return lax.ppermute(block, axis, [(i, i ^ mask) for i in range(lax.axis_size(axis))])


def iota(shape, dim):
    return lax.broadcasted_iota(jnp.int32, shape, dim)


def elu_wide(x):
    low = jnp.minimum(x, 0.0)
    series = 1.0 + low / 6.0
    for order in (5.0, 4.0, 3.0, 2.0):
        series = 1.0 + (low / order) * series
    below = jnp.where(low > -0.25, low * series, jnp.exp(low) - 1.0)
    return jnp.where(x > 0, x, below)


def start_below(position, lengths_ref):
    best = jnp.zeros_like(position)
    start = jnp.int32(0)
    for book in range(lengths_ref.shape[0]):
        best = jnp.where(start <= position, jnp.maximum(best, start), best)
        start = start + lengths_ref[book]
    return best


def ranks_of(owner_rows, seq_count):
    blocks, frames = owner_rows.shape
    parts = [
        (iota((seq_count, frames), 0) == owner_rows[b : b + 1].astype(jnp.int32)).astype(F32)
        for b in range(blocks)
    ]
    named = jnp.concatenate(parts, axis=0)
    before = (iota((frames, frames), 0) < iota((frames, frames), 1)).astype(BF16)
    counted = jnp.dot(named.astype(BF16), before, preferred_element_type=F32) * named
    return jnp.concatenate(
        [
            jnp.sum(counted[b * seq_count : (b + 1) * seq_count], axis=0, keepdims=True)
            for b in range(blocks)
        ],
        axis=0,
    )


def encode_kernel(piece, capacity, lengths_ref, feat_ref, edge_ref, owner_ref, w_ref, *rest):
    out_refs, padded = rest[:-1], rest[-1]
    frames, channels = feat_ref.shape
    taps = w_ref.shape[0]
    seq_count = 2 * len(out_refs)
    me = lax.axis_index("seq")
    edge = elu_wide(edge_ref[...].astype(F32)).astype(BF16).astype(F32)
    padded[0:8, :] = edge[edge.shape[0] - 8 :, :]
    padded[8:, :] = elu_wide(feat_ref[...].astype(F32)).astype(BF16).astype(F32)
    position = me * frames + iota((frames, 1), 0)
    start_of = start_below(position, lengths_ref)
    total = jnp.zeros((frames, w_ref.shape[2]), F32)
    for tap in range(taps):
        window = padded[8 - tap : 8 - tap + frames, :]
        window = jnp.where(position - tap >= start_of, window, 0.0).astype(BF16)
        total = total + jnp.dot(window, w_ref[tap], preferred_element_type=F32)
    latent = total.astype(BF16)
    owner = owner_ref[...]
    rank = ranks_of(owner, seq_count).astype(jnp.int32)
    row = jnp.bitwise_xor(owner, me) * piece + rank
    placed = (iota((seq_count * piece, frames), 0) == row).astype(F32).astype(BF16)
    outgoing = jnp.dot(placed, latent, preferred_element_type=F32)
    named = owner.astype(F32)
    if outgoing.shape[1] > frames:
        named = jnp.concatenate([named, jnp.zeros((1, outgoing.shape[1] - frames), F32)], axis=1)
    last = iota((seq_count * piece, 1), 0) % piece == piece - 1
    outgoing = jnp.where(last, named, outgoing).astype(BF16)
    for far, out_ref in enumerate(out_refs):
        out_ref[...] = outgoing[2 * far * piece : 2 * (far + 1) * piece]


def middle_kernel(piece, capacity, frames, count, *refs):
    far_count = count // 2
    latents = refs[:far_count]
    near = refs[far_count]
    w_refs = refs[far_count + 1 : far_count + 9]
    gain_ref, cot_ref, back_ref, hg_ref, arrived_ref, owners_ref = refs[far_count + 9 : far_count + 15]
    gathered, w_full, hidden, back = refs[far_count + 15 :]
    slots, width = cot_ref.shape
    rows = back_ref.shape[0]
    latent_width = back_ref.shape[1]
    seq, book = lax.axis_index("seq"), lax.axis_index("book")
    for far in range(far_count):
        gathered[2 * far * piece : (2 * far + 1) * piece, :] = latents[far][0:piece, :]
        gathered[(2 * far + 1) * piece : (2 * far + 2) * piece, :] = near[
            far * piece : (far + 1) * piece, :
        ]
    for rel in range(count):
        line = gathered[rel * piece : (rel + 1) * piece, 0:frames].astype(F32)
        owners_ref[pl.ds(jnp.bitwise_xor(seq, rel), 1), :] = line[piece - 1 : piece, :]
    columns = w_refs[0].shape[1]
    for index, w_ref in enumerate(w_refs):
        near_seq, near_y, near_core = index & 1, (index >> 1) & 1, index >> 2
        for far in range(far_count):
            at = jnp.bitwise_xor(seq, 2 * far + near_seq) * 4 + jnp.bitwise_xor(
                book, near_y * 2 + near_core
            )
            w_full[pl.ds(pl.multiple_of(at * columns, columns), columns), :] = w_ref[far]
    slot = iota((rows, 1), 0)
    source = jnp.zeros_like(slot)
    for block in range(1, count):
        source = source + (slot >= block * capacity).astype(jnp.int32)
    wanted = jnp.bitwise_xor(source, seq) * piece + slot - source * capacity
    wanted = jnp.where(slot < slots, wanted, -1)
    picked = (iota((rows, count * piece), 1) == wanted).astype(F32).astype(BF16)
    arrived = jnp.dot(picked, gathered[...], preferred_element_type=F32).astype(BF16)
    arrived_ref[...] = arrived
    step = latent_width
    squares = jnp.zeros((slots, step), F32)
    crossed = jnp.zeros((slots, step), F32)
    for at in range(0, width, step):
        part = lax.dot_general(
            arrived, w_full[at : at + step, :], (((1,), (1,)), ((), ())), preferred_element_type=F32
        )[:slots]
        hidden[:, at : at + step] = part
        squares = squares + part * part
        scaled = cot_ref[:, at : at + step].astype(F32) * gain_ref[:, at : at + step]
        crossed = crossed + part * scaled
    inv = lax.rsqrt(jnp.sum(squares, axis=1, keepdims=True) / width + 1e-05)
    pull = inv * inv * (jnp.sum(crossed, axis=1, keepdims=True) / width)
    total = jnp.zeros((rows, latent_width), F32)
    for at in range(0, width, step):
        part = hidden[:, at : at + step]
        grad_out = cot_ref[:, at : at + step].astype(F32)
        scaled = grad_out * gain_ref[:, at : at + step]
        grad = inv * (scaled - part * pull)
        grad = jnp.concatenate([grad, jnp.zeros((rows - slots, step), F32)], axis=0).astype(BF16)
        hg_ref[:, at : at + step] = grad
        total = total + jnp.dot(grad, w_full[at : at + step, :], preferred_element_type=F32)
        line = slots + at // step
        back[line : line + 1, :] = jnp.sum(grad_out * (part * inv), axis=0, keepdims=True)
    back[0:slots, :] = total[:slots]
    for line in range(slots + width // step, rows):
        back[line : line + 1, :] = jnp.zeros((1, latent_width), F32)
    back_ref[...] = back[...].astype(BF16)


def chip_order(count):
    return [(y, near, far) for y in (0, 1) for near in (0, 1) for far in range(count // 2)]


def projection_kernel(count, hg_ref, arrived_ref, send_ref, keep_ref):
    seq, book = lax.axis_index("seq"), lax.axis_index("book")
    core = jnp.bitwise_and(book, 1)
    chip = seq * 2 + (book >> 1)
    half = send_ref.shape[1]
    arrived = arrived_ref[...]
    for place, (y, near, far) in enumerate(chip_order(count)):
        at = jnp.bitwise_xor(chip, (2 * far + near) * 2 + y)
        grad = hg_ref[:, pl.ds(pl.multiple_of(at * 2 * half, 2 * half), 2 * half)]
        part = lax.dot_general(
            grad, arrived, (((0,), (0,)), ((), ())), preferred_element_type=F32
        )
        low, high = part[:half], part[half:]
        send_ref[place] = jnp.where(core == 0, high, low).astype(BF16)
        keep_ref[place] = jnp.where(core == 0, low, high).astype(BF16)


def prepare_kernel(capacity, rows, orders, lengths_ref, owners_ref, *refs):
    f_refs = refs[: len(orders)]
    turned_ref, facts_ref = refs[len(orders) :]
    count, frames = owners_ref.shape
    me = lax.axis_index("seq")
    for f_ref, order in zip(f_refs, orders):
        for index, rel in enumerate(order):
            act = elu_wide(f_ref[index * frames : (index + 1) * frames, :].astype(F32))
            at = jnp.bitwise_xor(me, rel) * frames
            turned_ref[:, pl.ds(pl.multiple_of(at, frames), frames)] = act.T.astype(BF16)
    owners = owners_ref[...]
    ranks = ranks_of(owners, count)
    eye = (iota((frames, frames), 0) == iota((frames, frames), 1)).astype(BF16)
    dims = (((1,), (1,)), ((), ()))
    owner_cols = lax.dot_general(eye, owners.astype(BF16), dims, preferred_element_type=F32)
    rank_cols = lax.dot_general(eye, ranks.astype(BF16), dims, preferred_element_type=F32)
    lane = iota((frames, facts_ref.shape[1]), 1)
    for block in range(count):
        owner = owner_cols[:, block : block + 1].astype(jnp.int32)
        rank = rank_cols[:, block : block + 1].astype(jnp.int32)
        slot = jnp.bitwise_xor(owner, me) * rows + block * capacity + rank
        position = block * frames + iota((frames, 1), 0)
        facts = slot
        for tap in range(1, facts_ref.shape[1]):
            later = position + tap
            valid = (later < count * frames) & (position >= start_below(later, lengths_ref))
            facts = jnp.where(lane == tap, valid.astype(jnp.int32), facts)
        facts_ref[block * frames : (block + 1) * frames, :] = facts


def spread_kernel(count, frames, taps, *refs):
    backs = refs[:count]
    facts_ref, turned_ref, send_ref, windows_ref, gain_ref, gathered, wide = refs[count:]
    rows, latent_width = backs[0].shape
    share = turned_ref.shape[0] // 4
    gain_rows = gain_ref.shape[0]
    book = lax.axis_index("book")
    gain = jnp.zeros((gain_rows, latent_width), F32)
    for rel, back_ref in enumerate(backs):
        gathered[rel * rows : (rel + 1) * rows, :] = back_ref[...]
        gain = gain + back_ref[...].astype(F32)[rows - gain_rows :]
    gain_ref[...] = gain
    for block in range(count):
        here = slice(block * frames, (block + 1) * frames)
        placed = iota((frames, count * rows), 1) == facts_ref[here, 0:1]
        wide[here, :] = jnp.dot(
            placed.astype(F32).astype(BF16), gathered[...], preferred_element_type=F32
        )
    wide[count * frames :, :] = jnp.zeros((8, latent_width), F32)
    for block in range(count):
        here = slice(block * frames, (block + 1) * frames)
        windows_ref[here, 0:latent_width] = wide[here, :].astype(BF16)
        for tap in range(1, taps):
            later = wide[block * frames + tap : (block + 1) * frames + tap, :]
            later = jnp.where(facts_ref[here, tap : tap + 1] > 0, later, 0.0)
            windows_ref[here, tap * latent_width : (tap + 1) * latent_width] = later.astype(BF16)
    part = kernel_part(turned_ref, windows_ref, book, share, 1)
    for y in (0, 1):
        for tap in range(taps):
            at = (y * taps + tap) * share
            send_ref[at : at + share, :] = part[
                y * share : (y + 1) * share, tap * latent_width : (tap + 1) * latent_width
            ].astype(BF16)
    high = gain.astype(BF16)
    at = 2 * taps * share
    send_ref[at : at + 2 * gain_rows, :] = jnp.concatenate(
        [high.astype(F32), gain - high.astype(F32)], axis=0
    ).astype(BF16)


def kernel_part(turned_ref, windows_ref, book, share, core):
    blocks = []
    for y in (0, 1):
        at = jnp.bitwise_xor(book, 2 * y + core) * share
        blocks.append(turned_ref[pl.ds(pl.multiple_of(at, share), share), :])
    return jnp.dot(
        jnp.concatenate(blocks, axis=0), windows_ref[...], preferred_element_type=F32
    )


def own_part_kernel(taps, turned_ref, windows_ref, out_ref):
    share, latent_width = turned_ref.shape[0] // 4, out_ref.shape[1]
    part = kernel_part(turned_ref, windows_ref, lax.axis_index("book"), share, 0)
    for y in (0, 1):
        for tap in range(taps):
            at = (y * taps + tap) * share
            out_ref[at : at + share, :] = part[
                y * share : (y + 1) * share, tap * latent_width : (tap + 1) * latent_width
            ]


def fold_kernel(kept_ref, got_ref, gain_ref, send_ref, mine_ref, gain_out_ref):
    half, gain_rows = mine_ref.shape[0], gain_ref.shape[0]
    mine_ref[...] = kept_ref[0:half, :] + got_ref[0:half, :].astype(F32)
    send_ref[0:half, :] = (
        kept_ref[half : 2 * half, :] + got_ref[half : 2 * half, :].astype(F32)
    ).astype(BF16)
    pair = got_ref[2 * half : 2 * half + 2 * gain_rows, :].astype(F32)
    gain = gain_ref[...] + (pair[:gain_rows] + pair[gain_rows:])
    gain_out_ref[...] = gain
    high = gain.astype(BF16).astype(F32)
    send_ref[half : half + 2 * gain_rows, :] = jnp.concatenate(
        [high, gain - high], axis=0
    ).astype(BF16)


def feature_kernel(feat_ref, windows_ref, w_ref, out_ref):
    frames = feat_ref.shape[0]
    taps, _, latent_width = w_ref.shape
    at = pl.multiple_of(lax.axis_index("seq") * frames, frames)
    total = jnp.zeros(feat_ref.shape, F32)
    for tap in range(taps):
        window = windows_ref[
            pl.ds(at, frames), tap * latent_width : (tap + 1) * latent_width
        ]
        total = total + lax.dot_general(
            window, w_ref[tap], (((1,), (1,)), ((), ())), preferred_element_type=F32
        )
    feats = feat_ref[...].astype(F32)
    slope = jnp.where(feats > 0, 1.0, jnp.exp(jnp.minimum(feats, 0.0)))
    out_ref[...] = (slope * total).astype(BF16)


def call(kernel, outs, operands, scratch=(), smem=0, flops=0):
    moved = sum(x.size * x.dtype.itemsize for x in (*outs, *operands))
    return pl.pallas_call(
        kernel,
        out_shape=outs,
        in_specs=[SMEM] * smem + [VMEM] * (len(operands) - smem),
        out_specs=jax.tree.map(lambda _: VMEM, outs),
        scratch_shapes=list(scratch),
        compiler_params=pltpu.CompilerParams(vmem_limit_bytes=24 * 2**20),
        cost_estimate=pl.CostEstimate(flops=flops, bytes_accessed=moved, transcendentals=0),
    )(*operands)


def shape(dims, dtype=BF16):
    return jax.ShapeDtypeStruct(dims, dtype)


def per_device(features, lengths, owner, w_enc, w_in, gain, cotangent):
    feats = features[0]
    cot = cotangent[0]
    book_lengths = lengths[0]
    frames, channels = feats.shape
    taps, _, latent_width = w_enc.shape
    slots, width = cot.shape
    count = lax.axis_size("seq")
    far_count = count // 2
    fars = range(1, far_count)
    capacity = max(2, frames // count + 1)
    piece = round_up(capacity + 1, 16)
    gain_rows = width // latent_width
    rows = round_up(slots + gain_rows, 16)
    share = channels // 4

    edge = shifted(feats[frames - 16 :], "seq", 1)
    w_own = w_in.T
    w_far = [w_own] + [swap(w_own, "seq", 2 * far) for far in fars]
    w_line = jnp.stack(w_far)
    w_near = swap(w_line, "seq", 1)
    w_side = swap(w_line, "book", 2)
    w_diag = swap(w_line, ("seq", "book"), 4 + 2)
    w_chips = [w_line, w_near, w_side, w_diag]
    w_pieces = w_chips + [swap(block, "book", 1) for block in w_chips]

    sent = call(
        functools.partial(encode_kernel, piece, capacity),
        [shape((2 * piece, latent_width))] * far_count,
        (book_lengths, feats, edge, owner[0].T, w_enc),
        scratch=[pltpu.VMEM((8 + frames, channels), F32)],
        smem=1,
    )
    landed = [sent[0]] + [swap(sent[far], "seq", 2 * far) for far in fars]
    near = swap(jnp.concatenate([block[piece:] for block in landed]), "seq", 1)

    back, hidden_grad, arrived, owners = call(
        functools.partial(middle_kernel, piece, capacity, frames, count),
        [
            shape((rows, latent_width)),
            shape((rows, width)),
            shape((rows, latent_width)),
            shape((count, frames), F32),
        ],
        (*landed, near, *w_pieces, gain[None], cot),
        scratch=[
            pltpu.VMEM((count * piece, latent_width), BF16),
            pltpu.VMEM((width, latent_width), BF16),
            pltpu.VMEM((slots, width), F32),
            pltpu.VMEM((rows, latent_width), F32),
        ],
    )
    backs = [back] + [swap(back, "seq", rel) for rel in range(1, count)]

    gathered, orders, mask, held, order = [feats], [[0]], far_count, feats, [0]
    while mask:
        got = swap(held, "seq", mask)
        gathered.append(got)
        orders.append([rel ^ mask for rel in order])
        order = order + orders[-1]
        mask //= 2
        if mask:
            held = jnp.concatenate([held, got])

    w_send, w_keep = call(
        functools.partial(projection_kernel, count),
        [shape((2 * count, w_in.shape[1], latent_width))] * 2,
        (hidden_grad, arrived),
    )
    w_sum = w_keep.astype(F32) + swap(w_send, "book", 1).astype(F32)
    w_sum = w_sum[:count] + swap(w_sum[count:].astype(BF16), "book", 2).astype(F32)
    w_sum = w_sum[:far_count] + swap(w_sum[far_count:].astype(BF16), "seq", 1).astype(F32)
    w_total = w_sum[0]
    for far in fars:
        w_total = w_total + swap(w_sum[far].astype(BF16), "seq", 2 * far).astype(F32)

    turned, facts = call(
        functools.partial(prepare_kernel, capacity, rows, orders),
        [shape((channels, count * frames)), shape((count * frames, taps), jnp.int32)],
        (book_lengths, owners, *gathered),
        smem=1,
    )
    message = 2 * taps * share + 2 * gain_rows
    k_send, windows, gain_seq = call(
        functools.partial(spread_kernel, count, frames, taps),
        [
            shape((message, latent_width)),
            shape((count * frames, taps * latent_width)),
            shape((gain_rows, latent_width), F32),
        ],
        (*backs, facts, turned),
        scratch=[
            pltpu.VMEM((count * rows, latent_width), BF16),
            pltpu.VMEM((count * frames + 8, latent_width), F32),
        ],
    )
    k_got = swap(k_send, "book", 1)
    (k_kept,) = call(
        functools.partial(own_part_kernel, taps),
        [shape((2 * taps * share, latent_width), F32)],
        (turned, windows),
    )
    y_send, k_mine, gain_pair = call(
        fold_kernel,
        [
            shape((taps * share + 2 * gain_rows, latent_width)),
            shape((taps * share, latent_width), F32),
            shape((gain_rows, latent_width), F32),
        ],
        (k_kept, k_got, gain_seq),
    )
    y_got = swap(y_send, "book", 2)
    (feature_grad,) = call(feature_kernel, [shape(feats.shape)], (feats, windows, w_enc))
    y_wide = y_got.astype(F32)
    kernel_mine = k_mine + y_wide[: taps * share]
    tail = y_wide[taps * share :]
    gain_total = (gain_pair + (tail[:gain_rows] + tail[gain_rows:])).reshape(width)
    return (
        feature_grad[None],
        kernel_mine.reshape(taps, share, latent_width),
        w_total.T,
        gain_total,
    )


def fits(mesh):
    count = mesh.shape["seq"]
    return mesh.shape["book"] == 4 and count in (2, 4, 8)


def solution(mesh):
    placed = (
        P("book", "seq", None),
        P("book", None),
        P("book", "seq", None),
        P(),
        P(None, ("seq", "book")),
        P(),
        P("book", "seq", None),
    )
    return jax.shard_map(
        per_device if fits(mesh) else per_device_gather,
        mesh=mesh,
        in_specs=placed,
        out_specs=(P("book", "seq", None), P(None, "book", None), P(None, ("seq", "book")), P()),
        check_vma=False,
    )
```

```python
import functools

import jax
import jax.numpy as jnp
from jax import lax
from jax.experimental import pallas as pl
from jax.experimental.pallas import tpu as pltpu
from jax.sharding import PartitionSpec as P

F32 = jnp.float32
BF16 = jnp.bfloat16
HEAVY = 20000000000
VMEM = pl.BlockSpec(memory_space=pltpu.VMEM)
SMEM = pl.BlockSpec(memory_space=pltpu.SMEM)


def shifted(block, axis, distance):
    devices = range(lax.axis_size(axis))
    route = [(i - distance, i) for i in devices if i - distance in devices]
    return lax.ppermute(block, axis, route)


def book_mask(position, book_lengths, offset):
    starts = jnp.cumsum(book_lengths) - book_lengths
    start_of = jnp.max(jnp.where(starts[None, :] <= position[:, None], starts[None, :], 0), axis=1)
    return position - offset >= start_of


def per_device_gather(features, lengths, owner, w_enc, w_in, gain, cotangent):
    feature_rows = features[0]
    frames, channels = feature_rows.shape
    tap_count, _, latent_width = w_enc.shape
    seq_count = lax.axis_size("seq")
    book_count = lax.axis_size("book")
    capacity = max(2, frames // seq_count + 1)
    first_frame = lax.axis_index("seq") * frames
    position = first_frame + jnp.arange(frames + tap_count - 1, dtype=jnp.int32)
    tap_masks = [book_mask(position, lengths[0], offset) for offset in range(tap_count)]
    feats_wide = feature_rows.astype(jnp.float32)
    activated = jax.nn.elu(feats_wide).astype(jnp.bfloat16)
    left_edge = shifted(activated[frames - (tap_count - 1) :], "seq", 1)
    padded = jnp.concatenate([left_edge, activated], axis=0)
    tap_inputs = []
    for offset in range(tap_count):
        begin = tap_count - 1 - offset
        window = padded[begin : begin + frames]
        tap_inputs.append(
            jnp.where(tap_masks[offset][:frames, None], window, jnp.zeros_like(window))
        )
    stacked = jnp.concatenate(tap_inputs, axis=1)
    latent = jnp.dot(
        stacked,
        w_enc.reshape(tap_count * channels, latent_width),
        preferred_element_type=jnp.float32,
    ).astype(jnp.bfloat16)
    owner_rank = owner[0, :, 0]
    one_hot = (owner_rank[:, None] == jnp.arange(seq_count, dtype=jnp.int32)[None, :]).astype(
        jnp.int32
    )
    slot_rank = jnp.sum((jnp.cumsum(one_hot, axis=0) - one_hot) * one_hot, axis=1)
    slot_index = owner_rank * capacity + slot_rank
    placement = (
        slot_index[:, None] == jnp.arange(seq_count * capacity, dtype=jnp.int32)[None, :]
    ).astype(jnp.bfloat16)
    outgoing = lax.dot_general(
        placement, latent, (((0,), (0,)), ((), ())), preferred_element_type=jnp.float32
    ).astype(jnp.bfloat16)
    arrived = lax.all_to_all(
        outgoing.reshape(seq_count, capacity, latent_width),
        "seq",
        split_axis=0,
        concat_axis=0,
        tiled=True,
    )
    arrived = arrived.reshape(seq_count * capacity, latent_width)
    w_full = lax.all_gather(w_in, ("seq", "book"), axis=1, tiled=True)
    grad_out = cotangent[0].astype(jnp.float32)
    hidden = jnp.dot(arrived, w_full, preferred_element_type=jnp.float32)
    inv_rms = lax.rsqrt(jnp.mean(hidden * hidden, axis=1, keepdims=True) + 1e-05)
    normed = hidden * inv_rms
    gain_term = grad_out * gain[None, :]
    hidden_grad = (
        inv_rms * (gain_term - normed * jnp.mean(gain_term * normed, axis=1, keepdims=True))
    ).astype(jnp.bfloat16)
    latent_back = lax.dot_general(
        hidden_grad, w_full, (((1,), (1,)), ((), ())), preferred_element_type=jnp.float32
    ).astype(jnp.bfloat16)
    w_part = lax.dot_general(
        arrived, hidden_grad, (((0,), (0,)), ((), ())), preferred_element_type=jnp.float32
    )
    gain_part = jnp.sum(grad_out * normed, axis=0)
    returned = lax.all_to_all(
        latent_back.reshape(seq_count, capacity, latent_width),
        "seq",
        split_axis=0,
        concat_axis=0,
        tiled=True,
    )
    returned = returned.reshape(seq_count * capacity, latent_width)
    latent_grad = jnp.dot(placement, returned, preferred_element_type=jnp.float32).astype(
        jnp.bfloat16
    )
    right_edge = shifted(latent_grad[: tap_count - 1], "seq", -1)
    extended = jnp.concatenate([latent_grad, right_edge], axis=0)
    tap_grads = []
    for offset in range(tap_count):
        window = extended[offset : offset + frames]
        tap_grads.append(
            jnp.where(
                tap_masks[offset][offset : offset + frames, None], window, jnp.zeros_like(window)
            )
        )
    kernel_back = jnp.transpose(w_enc, (0, 2, 1)).reshape(tap_count * latent_width, channels)
    activ_grad = jnp.dot(
        jnp.concatenate(tap_grads, axis=1), kernel_back, preferred_element_type=jnp.float32
    )
    slope = jnp.where(feats_wide > 0, 1.0, jnp.exp(feats_wide))
    feature_grad = (slope * activ_grad).astype(jnp.bfloat16)
    kernel_part = lax.dot_general(
        stacked, latent_grad, (((0,), (0,)), ((), ())), preferred_element_type=jnp.float32
    )
    kernel_part = kernel_part.reshape(tap_count, channels, latent_width)
    kernel_total, gain_total = lax.psum((kernel_part, gain_part), ("seq", "book"))
    share_width = channels // book_count
    kernel_mine = lax.dynamic_slice_in_dim(
        kernel_total, lax.axis_index("book") * share_width, share_width, 1
    )
    columns = w_in.shape[1]
    split_grad = w_part.reshape(latent_width, seq_count, book_count * columns)
    split_grad = lax.psum_scatter(
        split_grad.astype(jnp.bfloat16), "book", scatter_dimension=2, tiled=True
    ).astype(jnp.float32)
    w_grad = lax.psum_scatter(split_grad, "seq", scatter_dimension=1, tiled=True).reshape(
        latent_width, columns
    )
    return (feature_grad[None], kernel_mine, w_grad, gain_total)


def round_up(value, unit):
    return -(-value // unit) * unit


def swap(block, axis, mask):
    return lax.ppermute(block, axis, [(i, i ^ mask) for i in range(lax.axis_size(axis))])


def iota(shape, dim):
    return lax.broadcasted_iota(jnp.int32, shape, dim)


def elu_wide(x):
    low = jnp.minimum(x, 0.0)
    series = 1.0 + low / 6.0
    for order in (5.0, 4.0, 3.0, 2.0):
        series = 1.0 + (low / order) * series
    below = jnp.where(low > -0.25, low * series, jnp.exp(low) - 1.0)
    return jnp.where(x > 0, x, below)


def start_below(position, lengths_ref):
    best = jnp.zeros_like(position)
    start = jnp.int32(0)
    for book in range(lengths_ref.shape[0]):
        best = jnp.where(start <= position, jnp.maximum(best, start), best)
        start = start + lengths_ref[book]
    return best


def ranks_of(owner_rows, seq_count):
    blocks, frames = owner_rows.shape
    parts = [
        (iota((seq_count, frames), 0) == owner_rows[b : b + 1].astype(jnp.int32)).astype(F32)
        for b in range(blocks)
    ]
    named = jnp.concatenate(parts, axis=0)
    before = (iota((frames, frames), 0) < iota((frames, frames), 1)).astype(BF16)
    counted = jnp.dot(named.astype(BF16), before, preferred_element_type=F32) * named
    return jnp.concatenate(
        [
            jnp.sum(counted[b * seq_count : (b + 1) * seq_count], axis=0, keepdims=True)
            for b in range(blocks)
        ],
        axis=0,
    )


def activate_kernel(feat_ref, padded_ref, mine_ref, other_ref, turned):
    frames, channels = feat_ref.shape
    near = jnp.bitwise_and(lax.axis_index("seq"), 1)
    act = elu_wide(feat_ref[...].astype(F32)).astype(BF16).astype(F32)
    padded_ref[0:8, :] = jnp.zeros((8, channels), F32)
    padded_ref[8 : 8 + frames, :] = act
    padded_ref[8 + frames :, :] = jnp.zeros((16, channels), F32)
    turned[...] = act.T
    half = mine_ref.shape[0] // 4
    for book in range(4):
        for out_ref, side in ((mine_ref, near), (other_ref, 1 - near)):
            at = pl.multiple_of((2 * book + side) * half, half)
            out_ref[book * half : (book + 1) * half, :] = turned[pl.ds(at, half), :].astype(BF16)


def encode_kernel(
    piece, lengths_ref, padded, owner_ref, w_ref, total_ref, placed_ref, edge_ref, named_ref
):
    frames = total_ref.shape[0]
    taps = w_ref.shape[0]
    me = lax.axis_index("seq")
    seq_count = placed_ref.shape[0] // piece
    owner = owner_ref[...]
    rank = ranks_of(owner, seq_count).astype(jnp.int32)
    row = jnp.bitwise_xor(owner, me) * piece + rank
    placed_ref[...] = (iota((seq_count * piece, frames), 0) == row).astype(F32).astype(BF16)
    named = owner.astype(F32)
    if named_ref.shape[1] > frames:
        named = jnp.concatenate([named, jnp.zeros((1, named_ref.shape[1] - frames), F32)], axis=1)
    named_ref[...] = named
    position = me * frames + iota((frames, 1), 0)
    start_of = start_below(position, lengths_ref)
    after = (me + 1) * frames + iota((16, 1), 0)
    start_after = start_below(after, lengths_ref)
    total = jnp.zeros(total_ref.shape, F32)
    edge = jnp.zeros((16, total.shape[1]), F32)
    for tap in range(taps):
        window = padded[8 - tap : 8 - tap + frames, :]
        window = jnp.where(position - tap >= start_of, window, 0.0).astype(BF16)
        total = total + jnp.dot(window, w_ref[tap], preferred_element_type=F32)
        if tap:
            window = padded[8 + frames - tap : 24 + frames - tap, :]
            window = jnp.where(after - tap >= start_after, window, 0.0).astype(BF16)
            edge = edge + jnp.dot(window, w_ref[tap], preferred_element_type=F32)
    total_ref[...] = total
    edge_ref[...] = edge[: edge_ref.shape[0]]


def place_kernel(piece, total_ref, edge_ref, placed_ref, named_ref, *out_refs):
    seq_count = 2 * len(out_refs)
    lines = edge_ref.shape[0]
    total = total_ref[...]
    latent = jnp.concatenate([total[:lines] + edge_ref[...], total[lines:]], axis=0).astype(BF16)
    outgoing = jnp.dot(placed_ref[...], latent, preferred_element_type=F32)
    last = iota((seq_count * piece, 1), 0) % piece == piece - 1
    outgoing = jnp.where(last, named_ref[...], outgoing).astype(BF16)
    for far, out_ref in enumerate(out_refs):
        out_ref[...] = outgoing[2 * far * piece : 2 * (far + 1) * piece]


def join_rows_kernel(skip, *refs):
    rows = refs[0].shape[0] - skip
    for index, ref in enumerate(refs[:-1]):
        refs[-1][index * rows : (index + 1) * rows, :] = ref[skip:, :]


def middle_kernel(piece, capacity, frames, count, columns, *refs):
    far_count = count // 2
    landed, near = refs[:far_count], refs[far_count]
    w_refs = refs[far_count + 1 : far_count + 9]
    gain_ref, cot_ref, back_ref, hg_ref, arrived_ref, owners_ref = refs[far_count + 9 : far_count + 15]
    gathered, w_full, hidden, back = refs[far_count + 15 :]
    slots, width = cot_ref.shape
    rows = back_ref.shape[0]
    latent_width = back_ref.shape[1]
    seq, book = lax.axis_index("seq"), lax.axis_index("book")
    for far in range(far_count):
        gathered[2 * far * piece : (2 * far + 1) * piece, :] = landed[far][0:piece, :]
        gathered[(2 * far + 1) * piece : (2 * far + 2) * piece, :] = near[
            far * piece : (far + 1) * piece, :
        ]
    for rel in range(count):
        line = gathered[rel * piece : (rel + 1) * piece, 0:frames].astype(F32)
        owners_ref[pl.ds(jnp.bitwise_xor(seq, rel), 1), :] = line[piece - 1 : piece, :]
    for index, w_ref in enumerate(w_refs):
        near_seq, near_y, near_core = index & 1, (index >> 1) & 1, index >> 2
        for far in range(far_count):
            at = jnp.bitwise_xor(seq, 2 * far + near_seq) * 4 + jnp.bitwise_xor(
                book, near_y * 2 + near_core
            )
            w_full[pl.ds(pl.multiple_of(at * columns, columns), columns), :] = w_ref[
                far * columns : (far + 1) * columns, :
            ]
    slot = iota((rows, 1), 0)
    source = jnp.zeros_like(slot)
    for block in range(1, count):
        source = source + (slot >= block * capacity).astype(jnp.int32)
    wanted = jnp.bitwise_xor(source, seq) * piece + slot - source * capacity
    wanted = jnp.where(slot < slots, wanted, -1)
    picked = (iota((rows, count * piece), 1) == wanted).astype(F32).astype(BF16)
    arrived = jnp.dot(picked, gathered[...], preferred_element_type=F32).astype(BF16)
    arrived_ref[...] = arrived
    step = latent_width
    squares = jnp.zeros((slots, step), F32)
    crossed = jnp.zeros((slots, step), F32)
    for at in range(0, width, step):
        part = lax.dot_general(
            arrived, w_full[at : at + step, :], (((1,), (1,)), ((), ())), preferred_element_type=F32
        )[:slots]
        hidden[:, at : at + step] = part
        squares = squares + part * part
        scaled = cot_ref[:, at : at + step].astype(F32) * gain_ref[:, at : at + step]
        crossed = crossed + part * scaled
    inv = lax.rsqrt(jnp.sum(squares, axis=1, keepdims=True) / width + 1e-05)
    pull = inv * inv * (jnp.sum(crossed, axis=1, keepdims=True) / width)
    total = jnp.zeros((rows, latent_width), F32)
    for at in range(0, width, step):
        part = hidden[:, at : at + step]
        grad_out = cot_ref[:, at : at + step].astype(F32)
        scaled = grad_out * gain_ref[:, at : at + step]
        grad = inv * (scaled - part * pull)
        grad = jnp.concatenate([grad, jnp.zeros((rows - slots, step), F32)], axis=0).astype(BF16)
        hg_ref[:, at : at + step] = grad
        total = total + jnp.dot(grad, w_full[at : at + step, :], preferred_element_type=F32)
        line = slots + at // step
        back[line : line + 1, :] = jnp.sum(grad_out * (part * inv), axis=0, keepdims=True)
    back[0:slots, :] = total[:slots]
    for line in range(slots + width // step, rows):
        back[line : line + 1, :] = jnp.zeros((1, latent_width), F32)
    back_ref[...] = back[...].astype(BF16)


def chip_order(count):
    return [(y, near, far) for y in (0, 1) for near in (0, 1) for far in range(count // 2)]


def projection_kernel(count, hg_ref, arrived_ref, send_ref, keep_ref):
    seq, book = lax.axis_index("seq"), lax.axis_index("book")
    core = jnp.bitwise_and(book, 1)
    chip = seq * 2 + (book >> 1)
    half = send_ref.shape[1]
    arrived = arrived_ref[...]
    for place, (y, near, far) in enumerate(chip_order(count)):
        at = jnp.bitwise_xor(chip, (2 * far + near) * 2 + y)
        grad = hg_ref[:, pl.ds(pl.multiple_of(at * 2 * half, 2 * half), 2 * half)]
        part = lax.dot_general(
            grad, arrived, (((0,), (0,)), ((), ())), preferred_element_type=F32
        )
        low, high = part[:half], part[half:]
        send_ref[place] = jnp.where(core == 0, high, low).astype(BF16)
        keep_ref[place] = jnp.where(core == 0, low, high).astype(BF16)


def prepare_kernel(capacity, rows, lengths_ref, owners_ref, facts_ref):
    count, frames = owners_ref.shape
    taps = facts_ref.shape[1]
    me = lax.axis_index("seq")
    owners = owners_ref[...]
    ranks = ranks_of(owners, count)
    position = iota((count, frames), 0) * frames + iota((count, frames), 1)
    rows_of = [jnp.bitwise_xor(owners.astype(jnp.int32), me).astype(F32), ranks]
    for tap in range(1, taps):
        later = position + tap
        valid = (later < count * frames) & (position >= start_below(later, lengths_ref))
        rows_of.append(valid.astype(F32))
    eye = (iota((frames, frames), 0) == iota((frames, frames), 1)).astype(BF16)
    owner, rank, *valid = [
        lax.dot_general(
            eye, lines.astype(BF16), (((1,), (1,)), ((), ())), preferred_element_type=F32
        )
        for lines in rows_of
    ]
    lane = iota((frames, taps), 1)
    for block in range(count):
        here = slice(block, block + 1)
        facts = owner[:, here] * rows + (rank[:, here] + block * capacity)
        for tap in range(1, taps):
            facts = jnp.where(lane == tap, valid[tap - 1][:, here], facts)
        facts_ref[block * frames : (block + 1) * frames, :] = facts.astype(jnp.int32)


def spread_kernel(orders, count, frames, taps, *refs):
    backs, turned_refs = refs[:count], refs[count : count + len(orders)]
    facts_ref, send_ref, windows_ref, gain_ref, gathered, wide, lhs = refs[count + len(orders) :]
    rows, latent_width = backs[0].shape
    share = turned_refs[0].shape[1] // 4
    gain_rows = gain_ref.shape[0]
    gain = jnp.zeros((gain_rows, latent_width), F32)
    for rel, back_ref in enumerate(backs):
        gathered[rel * rows : (rel + 1) * rows, :] = back_ref[...]
        gain = gain + back_ref[...].astype(F32)[rows - gain_rows :]
    gain_ref[...] = gain
    for block in range(count):
        here = slice(block * frames, (block + 1) * frames)
        placed = iota((frames, count * rows), 1) == facts_ref[here, 0:1]
        wide[here, :] = jnp.dot(
            placed.astype(F32).astype(BF16), gathered[...], preferred_element_type=F32
        )
    wide[count * frames :, :] = jnp.zeros((8, latent_width), F32)
    for block in range(count):
        here = slice(block * frames, (block + 1) * frames)
        windows_ref[here, 0:latent_width] = wide[here, :].astype(BF16)
        for tap in range(1, taps):
            later = wide[block * frames + tap : (block + 1) * frames + tap, :]
            later = jnp.where(facts_ref[here, tap : tap + 1] > 0, later, 0.0)
            windows_ref[here, tap * latent_width : (tap + 1) * latent_width] = later.astype(BF16)
    part = kernel_part(orders, turned_refs, windows_ref, lhs, share, 1)
    for y in (0, 1):
        for tap in range(taps):
            at = (y * taps + tap) * share
            send_ref[at : at + share, :] = part[
                y * share : (y + 1) * share, tap * latent_width : (tap + 1) * latent_width
            ].astype(BF16)
    high = gain.astype(BF16)
    at = 2 * taps * share
    send_ref[at : at + 2 * gain_rows, :] = jnp.concatenate(
        [high.astype(F32), gain - high.astype(F32)], axis=0
    ).astype(BF16)


def kernel_part(orders, turned_refs, windows_ref, lhs, share, core):
    seq, book = lax.axis_index("seq"), lax.axis_index("book")
    for turned_ref, order in zip(turned_refs, orders):
        frames = turned_ref.shape[2]
        for index, rel in enumerate(order):
            lanes = pl.ds(pl.multiple_of(jnp.bitwise_xor(seq, rel) * frames, frames), frames)
            for y in (0, 1):
                at = jnp.bitwise_xor(book, 2 * y + core) * share
                lhs[y * share : (y + 1) * share, lanes] = turned_ref[
                    index, pl.ds(pl.multiple_of(at, share), share), :
                ]
    return jnp.dot(lhs[...], windows_ref[...], preferred_element_type=F32)


def own_part_kernel(orders, taps, *refs):
    turned_refs, (windows_ref, out_ref, lhs) = refs[: len(orders)], refs[len(orders) :]
    share, latent_width = turned_refs[0].shape[1] // 4, out_ref.shape[1]
    part = kernel_part(orders, turned_refs, windows_ref, lhs, share, 0)
    for y in (0, 1):
        for tap in range(taps):
            at = (y * taps + tap) * share
            out_ref[at : at + share, :] = part[
                y * share : (y + 1) * share, tap * latent_width : (tap + 1) * latent_width
            ]


def fold_kernel(kept_ref, got_ref, gain_ref, send_ref, mine_ref, gain_out_ref):
    half, gain_rows = mine_ref.shape[0], gain_ref.shape[0]
    mine_ref[...] = kept_ref[0:half, :] + got_ref[0:half, :].astype(F32)
    send_ref[0:half, :] = (
        kept_ref[half : 2 * half, :] + got_ref[half : 2 * half, :].astype(F32)
    ).astype(BF16)
    pair = got_ref[2 * half : 2 * half + 2 * gain_rows, :].astype(F32)
    gain = gain_ref[...] + (pair[:gain_rows] + pair[gain_rows:])
    gain_out_ref[...] = gain
    high = gain.astype(BF16).astype(F32)
    send_ref[half : half + 2 * gain_rows, :] = jnp.concatenate(
        [high, gain - high], axis=0
    ).astype(BF16)


def finish_kernel(mine_ref, got_ref, gain_ref, send_ref, out_ref, gain_out_ref):
    half, gain_rows = mine_ref.shape[0], gain_ref.shape[0]
    total = mine_ref[...] + got_ref[0:half, :].astype(F32)
    out_ref[...] = total
    send_ref[...] = total.astype(BF16)
    pair = got_ref[half : half + 2 * gain_rows, :].astype(F32)
    gain = gain_ref[...] + (pair[:gain_rows] + pair[gain_rows:])
    step = gain.shape[1]
    for line in range(gain_rows):
        gain_out_ref[:, line * step : (line + 1) * step] = gain[line : line + 1]


def join_kernel(mine_ref, got_ref, out_ref):
    taps, share = out_ref.shape[:2]
    half = share // 2
    near = jnp.bitwise_and(lax.axis_index("seq"), 1)
    for tap in range(taps):
        here = slice(tap * half, (tap + 1) * half)
        mine, got = mine_ref[here, :], got_ref[here, :].astype(F32)
        out_ref[tap, 0:half, :] = jnp.where(near == 0, mine, got)
        out_ref[tap, half:, :] = jnp.where(near == 0, got, mine)


def feature_kernel(feat_ref, windows_ref, w_ref, out_ref):
    frames = feat_ref.shape[0]
    taps, _, latent_width = w_ref.shape
    at = pl.multiple_of(lax.axis_index("seq") * frames, frames)
    total = jnp.zeros(feat_ref.shape, F32)
    for tap in range(taps):
        window = windows_ref[
            pl.ds(at, frames), tap * latent_width : (tap + 1) * latent_width
        ]
        total = total + lax.dot_general(
            window, w_ref[tap], (((1,), (1,)), ((), ())), preferred_element_type=F32
        )
    feats = feat_ref[...].astype(F32)
    slope = jnp.where(feats > 0, 1.0, jnp.exp(jnp.minimum(feats, 0.0)))
    out_ref[...] = (slope * total).astype(BF16)


def call(kernel, outs, operands, scratch=(), smem=0, flops=0):
    return pl.pallas_call(
        kernel,
        out_shape=outs,
        in_specs=[SMEM] * smem + [VMEM] * (len(operands) - smem),
        out_specs=jax.tree.map(lambda _: VMEM, outs),
        scratch_shapes=list(scratch),
        compiler_params=pltpu.CompilerParams(vmem_limit_bytes=24 * 2**20),
        cost_estimate=pl.CostEstimate(flops=flops, bytes_accessed=1024, transcendentals=0),
    )(*operands)


def shape(dims, dtype=BF16):
    return jax.ShapeDtypeStruct(dims, dtype)


def per_device(features, lengths, owner, w_enc, w_in, gain, cotangent):
    feats = features[0]
    cot = cotangent[0]
    book_lengths = lengths[0]
    frames, channels = feats.shape
    taps, _, latent_width = w_enc.shape
    slots, width = cot.shape
    count = lax.axis_size("seq")
    far_count = count // 2
    fars = range(1, far_count)
    capacity = max(2, frames // count + 1)
    piece = round_up(capacity + 1, 16)
    gain_rows = width // latent_width
    rows = round_up(slots + gain_rows, 16)
    half = channels // 8

    columns = w_in.shape[1]
    padded, mine, other = call(
        activate_kernel,
        [
            shape((24 + frames, channels), F32),
            shape((channels // 2, frames)),
            shape((channels // 2, frames)),
        ],
        (feats,),
        scratch=[pltpu.VMEM((channels, frames), F32)],
        flops=HEAVY // 10,
    )
    total, placed, edge, named = call(
        functools.partial(encode_kernel, piece),
        [
            shape((frames, latent_width), F32),
            shape((count * piece, frames)),
            shape((8, latent_width), F32),
            shape((1, latent_width), F32),
        ],
        (book_lengths, padded, owner[0].T, w_enc),
        smem=1,
    )
    w_own, edge, other = lax.optimization_barrier((w_in.T, edge, other))
    edge = shifted(edge, "seq", 1)
    w_far = [w_own] + [swap(w_own, "seq", 2 * far) for far in fars]
    held = jnp.stack([mine, swap(other, "seq", 1)])
    sent = call(
        functools.partial(place_kernel, piece),
        [shape((2 * piece, latent_width))] * far_count,
        (total, edge, placed, named),
    )
    w_far, held, sent = lax.optimization_barrier((w_far, held, sent))
    landed = [sent[0]] + [swap(sent[far], "seq", 2 * far) for far in fars]
    (w_line,) = call(
        functools.partial(join_rows_kernel, 0),
        [shape((far_count * columns, latent_width))],
        tuple(w_far),
        flops=HEAVY,
    )
    w_near = swap(w_line, "seq", 1)
    w_side = swap(w_line, "book", 2)
    w_diag = swap(w_line, ("seq", "book"), 4 + 2)
    got = swap(held, "seq", 4)
    (near,) = call(
        functools.partial(join_rows_kernel, piece),
        [shape((far_count * piece, latent_width))],
        tuple(landed),
        flops=HEAVY,
    )
    near = swap(near, "seq", 1)
    w_chips = [w_line, w_near, w_side, w_diag]
    w_chips, got = lax.optimization_barrier((w_chips, got))
    held = jnp.concatenate([held, got])
    w_pieces = w_chips + [swap(block, "book", 1) for block in w_chips]
    second = swap(held, "seq", 2)
    turned_all = [held, second]
    orders = [[0, 1, 4, 5], [2, 3, 6, 7]]

    back, hidden_grad, arrived, owners = call(
        functools.partial(middle_kernel, piece, capacity, frames, count, columns),
        [
            shape((rows, latent_width)),
            shape((rows, width)),
            shape((rows, latent_width)),
            shape((count, frames), F32),
        ],
        (*landed, near, *w_pieces, gain[None], cot),
        scratch=[
            pltpu.VMEM((count * piece, latent_width), BF16),
            pltpu.VMEM((width, latent_width), BF16),
            pltpu.VMEM((slots, width), F32),
            pltpu.VMEM((rows, latent_width), F32),
        ],
        flops=HEAVY,
    )
    backs = [back] + [swap(back, "seq", rel) for rel in range(1, count)]

    (facts,) = call(
        functools.partial(prepare_kernel, capacity, rows),
        [shape((count * frames, taps), jnp.int32)],
        (book_lengths, owners),
        smem=1,
        flops=HEAVY,
    )
    w_send, w_keep = call(
        functools.partial(projection_kernel, count),
        [shape((2 * count, columns, latent_width))] * 2,
        (hidden_grad, arrived),
    )
    w_got, facts = lax.optimization_barrier((swap(w_send, "book", 1), facts))
    w_sum = w_keep.astype(F32) + w_got.astype(F32)
    w_sum = w_sum[:count] + swap(w_sum[count:].astype(BF16), "book", 2).astype(F32)
    w_sum = w_sum[:far_count] + swap(w_sum[far_count:].astype(BF16), "seq", 1).astype(F32)
    w_total = w_sum[0]
    for far in fars:
        w_total = w_total + swap(w_sum[far].astype(BF16), "seq", 2 * far).astype(F32)

    message = 2 * taps * half + 2 * gain_rows
    k_send, windows, gain_seq = call(
        functools.partial(spread_kernel, orders, count, frames, taps),
        [
            shape((message, latent_width)),
            shape((count * frames, taps * latent_width)),
            shape((gain_rows, latent_width), F32),
        ],
        (*backs, *turned_all, facts),
        scratch=[
            pltpu.VMEM((count * rows, latent_width), BF16),
            pltpu.VMEM((count * frames + 8, latent_width), F32),
            pltpu.VMEM((2 * half, count * frames), BF16),
        ],
        flops=HEAVY,
    )
    k_got = swap(k_send, "book", 1)
    (k_kept,) = call(
        functools.partial(own_part_kernel, orders, taps),
        [shape((2 * taps * half, latent_width), F32)],
        (*turned_all, windows),
        scratch=[pltpu.VMEM((2 * half, count * frames), BF16)],
        flops=HEAVY,
    )
    y_send, k_mine, gain_pair = call(
        fold_kernel,
        [
            shape((taps * half + 2 * gain_rows, latent_width)),
            shape((taps * half, latent_width), F32),
            shape((gain_rows, latent_width), F32),
        ],
        (k_kept, k_got, gain_seq),
    )
    y_got = swap(y_send, "book", 2)
    (feature_grad,) = call(
        feature_kernel, [shape(feats.shape)], (feats, windows, w_enc), flops=HEAVY
    )
    y_got, feature_grad = lax.optimization_barrier((y_got, feature_grad))
    x_back, kernel_half, gain_total = call(
        finish_kernel,
        [
            shape((taps * half, latent_width)),
            shape((taps * half, latent_width), F32),
            shape((1, width), F32),
        ],
        (k_mine, y_got, gain_pair),
    )
    (kernel_mine,) = call(
        join_kernel,
        [shape((taps, 2 * half, latent_width), F32)],
        (kernel_half, swap(x_back, "seq", 1)),
    )
    return (
        feature_grad[None],
        kernel_mine,
        w_total.T,
        gain_total[0],
    )


def fits(mesh):
    count = mesh.shape["seq"]
    return mesh.shape["book"] == 4 and count in (2, 4, 8)


def solution(mesh):
    placed = (
        P("book", "seq", None),
        P("book", None),
        P("book", "seq", None),
        P(),
        P(None, ("seq", "book")),
        P(),
        P("book", "seq", None),
    )
    return jax.shard_map(
        per_device if fits(mesh) else per_device_gather,
        mesh=mesh,
        in_specs=placed,
        out_specs=(P("book", "seq", None), P(None, "book", None), P(None, ("seq", "book")), P()),
        check_vma=False,
    )
```

```python
import functools

import jax
import jax.numpy as jnp
from jax import lax
from jax.experimental import pallas as pl
from jax.experimental.pallas import tpu as pltpu
from jax.sharding import PartitionSpec as P

F32 = jnp.float32
BF16 = jnp.bfloat16
HEAVY = 20000000000
VMEM = pl.BlockSpec(memory_space=pltpu.VMEM)
SMEM = pl.BlockSpec(memory_space=pltpu.SMEM)


def shifted(block, axis, distance):
    devices = range(lax.axis_size(axis))
    route = [(i - distance, i) for i in devices if i - distance in devices]
    return lax.ppermute(block, axis, route)


def book_mask(position, book_lengths, offset):
    starts = jnp.cumsum(book_lengths) - book_lengths
    start_of = jnp.max(jnp.where(starts[None, :] <= position[:, None], starts[None, :], 0), axis=1)
    return position - offset >= start_of


def per_device_gather(features, lengths, owner, w_enc, w_in, gain, cotangent):
    feature_rows = features[0]
    frames, channels = feature_rows.shape
    tap_count, _, latent_width = w_enc.shape
    seq_count = lax.axis_size("seq")
    book_count = lax.axis_size("book")
    capacity = max(2, frames // seq_count + 1)
    first_frame = lax.axis_index("seq") * frames
    position = first_frame + jnp.arange(frames + tap_count - 1, dtype=jnp.int32)
    tap_masks = [book_mask(position, lengths[0], offset) for offset in range(tap_count)]
    feats_wide = feature_rows.astype(jnp.float32)
    activated = jax.nn.elu(feats_wide).astype(jnp.bfloat16)
    left_edge = shifted(activated[frames - (tap_count - 1) :], "seq", 1)
    padded = jnp.concatenate([left_edge, activated], axis=0)
    tap_inputs = []
    for offset in range(tap_count):
        begin = tap_count - 1 - offset
        window = padded[begin : begin + frames]
        tap_inputs.append(
            jnp.where(tap_masks[offset][:frames, None], window, jnp.zeros_like(window))
        )
    stacked = jnp.concatenate(tap_inputs, axis=1)
    latent = jnp.dot(
        stacked,
        w_enc.reshape(tap_count * channels, latent_width),
        preferred_element_type=jnp.float32,
    ).astype(jnp.bfloat16)
    owner_rank = owner[0, :, 0]
    one_hot = (owner_rank[:, None] == jnp.arange(seq_count, dtype=jnp.int32)[None, :]).astype(
        jnp.int32
    )
    slot_rank = jnp.sum((jnp.cumsum(one_hot, axis=0) - one_hot) * one_hot, axis=1)
    slot_index = owner_rank * capacity + slot_rank
    placement = (
        slot_index[:, None] == jnp.arange(seq_count * capacity, dtype=jnp.int32)[None, :]
    ).astype(jnp.bfloat16)
    outgoing = lax.dot_general(
        placement, latent, (((0,), (0,)), ((), ())), preferred_element_type=jnp.float32
    ).astype(jnp.bfloat16)
    arrived = lax.all_to_all(
        outgoing.reshape(seq_count, capacity, latent_width),
        "seq",
        split_axis=0,
        concat_axis=0,
        tiled=True,
    )
    arrived = arrived.reshape(seq_count * capacity, latent_width)
    w_full = lax.all_gather(w_in, ("seq", "book"), axis=1, tiled=True)
    grad_out = cotangent[0].astype(jnp.float32)
    hidden = jnp.dot(arrived, w_full, preferred_element_type=jnp.float32)
    inv_rms = lax.rsqrt(jnp.mean(hidden * hidden, axis=1, keepdims=True) + 1e-05)
    normed = hidden * inv_rms
    gain_term = grad_out * gain[None, :]
    hidden_grad = (
        inv_rms * (gain_term - normed * jnp.mean(gain_term * normed, axis=1, keepdims=True))
    ).astype(jnp.bfloat16)
    latent_back = lax.dot_general(
        hidden_grad, w_full, (((1,), (1,)), ((), ())), preferred_element_type=jnp.float32
    ).astype(jnp.bfloat16)
    w_part = lax.dot_general(
        arrived, hidden_grad, (((0,), (0,)), ((), ())), preferred_element_type=jnp.float32
    )
    gain_part = jnp.sum(grad_out * normed, axis=0)
    returned = lax.all_to_all(
        latent_back.reshape(seq_count, capacity, latent_width),
        "seq",
        split_axis=0,
        concat_axis=0,
        tiled=True,
    )
    returned = returned.reshape(seq_count * capacity, latent_width)
    latent_grad = jnp.dot(placement, returned, preferred_element_type=jnp.float32).astype(
        jnp.bfloat16
    )
    right_edge = shifted(latent_grad[: tap_count - 1], "seq", -1)
    extended = jnp.concatenate([latent_grad, right_edge], axis=0)
    tap_grads = []
    for offset in range(tap_count):
        window = extended[offset : offset + frames]
        tap_grads.append(
            jnp.where(
                tap_masks[offset][offset : offset + frames, None], window, jnp.zeros_like(window)
            )
        )
    kernel_back = jnp.transpose(w_enc, (0, 2, 1)).reshape(tap_count * latent_width, channels)
    activ_grad = jnp.dot(
        jnp.concatenate(tap_grads, axis=1), kernel_back, preferred_element_type=jnp.float32
    )
    slope = jnp.where(feats_wide > 0, 1.0, jnp.exp(feats_wide))
    feature_grad = (slope * activ_grad).astype(jnp.bfloat16)
    kernel_part = lax.dot_general(
        stacked, latent_grad, (((0,), (0,)), ((), ())), preferred_element_type=jnp.float32
    )
    kernel_part = kernel_part.reshape(tap_count, channels, latent_width)
    kernel_total, gain_total = lax.psum((kernel_part, gain_part), ("seq", "book"))
    share_width = channels // book_count
    kernel_mine = lax.dynamic_slice_in_dim(
        kernel_total, lax.axis_index("book") * share_width, share_width, 1
    )
    columns = w_in.shape[1]
    split_grad = w_part.reshape(latent_width, seq_count, book_count * columns)
    split_grad = lax.psum_scatter(
        split_grad.astype(jnp.bfloat16), "book", scatter_dimension=2, tiled=True
    ).astype(jnp.float32)
    w_grad = lax.psum_scatter(split_grad, "seq", scatter_dimension=1, tiled=True).reshape(
        latent_width, columns
    )
    return (feature_grad[None], kernel_mine, w_grad, gain_total)


def round_up(value, unit):
    return -(-value // unit) * unit


def swap(block, axis, mask):
    return lax.ppermute(block, axis, [(i, i ^ mask) for i in range(lax.axis_size(axis))])


def after(block, *others):
    return lax.optimization_barrier((block, *others))[0]


def iota(shape, dim):
    return lax.broadcasted_iota(jnp.int32, shape, dim)


def elu_wide(x):
    low = jnp.minimum(x, 0.0)
    series = 1.0 + low / 6.0
    for order in (5.0, 4.0, 3.0, 2.0):
        series = 1.0 + (low / order) * series
    below = jnp.where(low > -0.25, low * series, jnp.exp(low) - 1.0)
    return jnp.where(x > 0, x, below)


def start_below(position, lengths_ref):
    best = jnp.zeros_like(position)
    start = jnp.int32(0)
    for book in range(lengths_ref.shape[0]):
        best = jnp.where(start <= position, jnp.maximum(best, start), best)
        start = start + lengths_ref[book]
    return best


def ranks_of(owner_rows, seq_count):
    blocks, frames = owner_rows.shape
    parts = [
        (iota((seq_count, frames), 0) == owner_rows[b : b + 1].astype(jnp.int32)).astype(F32)
        for b in range(blocks)
    ]
    named = jnp.concatenate(parts, axis=0)
    before = (iota((frames, frames), 0) < iota((frames, frames), 1)).astype(BF16)
    counted = jnp.dot(named.astype(BF16), before, preferred_element_type=F32) * named
    return jnp.concatenate(
        [
            jnp.sum(counted[b * seq_count : (b + 1) * seq_count], axis=0, keepdims=True)
            for b in range(blocks)
        ],
        axis=0,
    )


def activate_kernel(feat_ref, padded_ref, turned_ref):
    frames, channels = feat_ref.shape
    act = elu_wide(feat_ref[...].astype(F32)).astype(BF16).astype(F32)
    padded_ref[0:8, :] = jnp.zeros((8, channels), F32)
    padded_ref[8 : 8 + frames, :] = act
    padded_ref[8 + frames :, :] = jnp.zeros((16, channels), F32)
    turned_ref[...] = act.T.astype(BF16)


def encode_kernel(
    piece, lengths_ref, padded, owner_ref, w_ref, total_ref, placed_ref, edge_ref, named_ref
):
    frames = total_ref.shape[0]
    taps = w_ref.shape[0]
    me = lax.axis_index("seq")
    seq_count = placed_ref.shape[0] // piece
    owner = owner_ref[...]
    rank = ranks_of(owner, seq_count).astype(jnp.int32)
    row = jnp.bitwise_xor(owner, me) * piece + rank
    placed_ref[...] = (iota((seq_count * piece, frames), 0) == row).astype(F32).astype(BF16)
    named = owner.astype(F32)
    if named_ref.shape[1] > frames:
        named = jnp.concatenate([named, jnp.zeros((1, named_ref.shape[1] - frames), F32)], axis=1)
    named_ref[...] = named
    position = me * frames + iota((frames, 1), 0)
    start_of = start_below(position, lengths_ref)
    beyond = (me + 1) * frames + iota((16, 1), 0)
    start_beyond = start_below(beyond, lengths_ref)
    total = jnp.zeros(total_ref.shape, F32)
    edge = jnp.zeros((16, total.shape[1]), F32)
    for tap in range(taps):
        window = padded[8 - tap : 8 - tap + frames, :]
        window = jnp.where(position - tap >= start_of, window, 0.0).astype(BF16)
        total = total + jnp.dot(window, w_ref[tap], preferred_element_type=F32)
        if tap:
            window = padded[8 + frames - tap : 24 + frames - tap, :]
            window = jnp.where(beyond - tap >= start_beyond, window, 0.0).astype(BF16)
            edge = edge + jnp.dot(window, w_ref[tap], preferred_element_type=F32)
    total_ref[...] = total
    edge_ref[...] = edge[: edge_ref.shape[0]]


def place_kernel(piece, total_ref, edge_ref, placed_ref, named_ref, *out_refs):
    seq_count = 2 * len(out_refs)
    lines = edge_ref.shape[0]
    total = total_ref[...]
    latent = jnp.concatenate([total[:lines] + edge_ref[...], total[lines:]], axis=0).astype(BF16)
    outgoing = jnp.dot(placed_ref[...], latent, preferred_element_type=F32)
    last = iota((seq_count * piece, 1), 0) % piece == piece - 1
    outgoing = jnp.where(last, named_ref[...], outgoing).astype(BF16)
    for far, out_ref in enumerate(out_refs):
        out_ref[...] = outgoing[2 * far * piece : 2 * (far + 1) * piece]


def join_rows_kernel(skip, *refs):
    rows = refs[0].shape[0] - skip
    for index, ref in enumerate(refs[:-1]):
        refs[-1][index * rows : (index + 1) * rows, :] = ref[skip:, :]


def middle_kernel(piece, capacity, frames, count, columns, *refs):
    far_count = count // 2
    landed, near = refs[:far_count], refs[far_count]
    w_refs = refs[far_count + 1 : far_count + 9]
    gain_ref, cot_ref, back_ref, hg_ref, arrived_ref, owners_ref = refs[far_count + 9 : far_count + 15]
    gathered, w_full, hidden, back = refs[far_count + 15 :]
    slots, width = cot_ref.shape
    rows = back_ref.shape[0]
    latent_width = back_ref.shape[1]
    seq, book = lax.axis_index("seq"), lax.axis_index("book")
    for far in range(far_count):
        gathered[2 * far * piece : (2 * far + 1) * piece, :] = landed[far][0:piece, :]
        gathered[(2 * far + 1) * piece : (2 * far + 2) * piece, :] = near[
            far * piece : (far + 1) * piece, :
        ]
    for rel in range(count):
        line = gathered[rel * piece : (rel + 1) * piece, 0:frames].astype(F32)
        owners_ref[pl.ds(jnp.bitwise_xor(seq, rel), 1), :] = line[piece - 1 : piece, :]
    for index, w_ref in enumerate(w_refs):
        near_seq, near_y, near_core = index & 1, (index >> 1) & 1, index >> 2
        for far in range(far_count):
            at = jnp.bitwise_xor(seq, 2 * far + near_seq) * 4 + jnp.bitwise_xor(
                book, near_y * 2 + near_core
            )
            w_full[pl.ds(pl.multiple_of(at * columns, columns), columns), :] = w_ref[
                far * columns : (far + 1) * columns, :
            ]
    slot = iota((rows, 1), 0)
    source = jnp.zeros_like(slot)
    for block in range(1, count):
        source = source + (slot >= block * capacity).astype(jnp.int32)
    wanted = jnp.bitwise_xor(source, seq) * piece + slot - source * capacity
    wanted = jnp.where(slot < slots, wanted, -1)
    picked = (iota((rows, count * piece), 1) == wanted).astype(F32).astype(BF16)
    arrived = jnp.dot(picked, gathered[...], preferred_element_type=F32).astype(BF16)
    arrived_ref[...] = arrived
    step = latent_width
    squares = jnp.zeros((slots, step), F32)
    crossed = jnp.zeros((slots, step), F32)
    for at in range(0, width, step):
        part = lax.dot_general(
            arrived, w_full[at : at + step, :], (((1,), (1,)), ((), ())), preferred_element_type=F32
        )[:slots]
        hidden[:, at : at + step] = part
        squares = squares + part * part
        scaled = cot_ref[:, at : at + step].astype(F32) * gain_ref[:, at : at + step]
        crossed = crossed + part * scaled
    inv = lax.rsqrt(jnp.sum(squares, axis=1, keepdims=True) / width + 1e-05)
    pull = inv * inv * (jnp.sum(crossed, axis=1, keepdims=True) / width)
    total = jnp.zeros((rows, latent_width), F32)
    for at in range(0, width, step):
        part = hidden[:, at : at + step]
        grad_out = cot_ref[:, at : at + step].astype(F32)
        scaled = grad_out * gain_ref[:, at : at + step]
        grad = inv * (scaled - part * pull)
        grad = jnp.concatenate([grad, jnp.zeros((rows - slots, step), F32)], axis=0).astype(BF16)
        hg_ref[:, at : at + step] = grad
        total = total + jnp.dot(grad, w_full[at : at + step, :], preferred_element_type=F32)
        line = slots + at // step
        back[line : line + 1, :] = jnp.sum(grad_out * (part * inv), axis=0, keepdims=True)
    back[0:slots, :] = total[:slots]
    for line in range(slots + width // step, rows):
        back[line : line + 1, :] = jnp.zeros((1, latent_width), F32)
    back_ref[...] = back[...].astype(BF16)


def chip_order(count):
    return [(y, near, far) for y in (0, 1) for near in (0, 1) for far in range(count // 2)]


def projection_kernel(count, hg_ref, arrived_ref, send_ref, keep_ref):
    seq, book = lax.axis_index("seq"), lax.axis_index("book")
    core = jnp.bitwise_and(book, 1)
    chip = seq * 2 + (book >> 1)
    half = send_ref.shape[1]
    arrived = arrived_ref[...]
    for place, (y, near, far) in enumerate(chip_order(count)):
        at = jnp.bitwise_xor(chip, (2 * far + near) * 2 + y)
        grad = hg_ref[:, pl.ds(pl.multiple_of(at * 2 * half, 2 * half), 2 * half)]
        part = lax.dot_general(
            grad, arrived, (((0,), (0,)), ((), ())), preferred_element_type=F32
        )
        low, high = part[:half], part[half:]
        send_ref[place] = jnp.where(core == 0, high, low).astype(BF16)
        keep_ref[place] = jnp.where(core == 0, low, high).astype(BF16)


def prepare_kernel(capacity, rows, lengths_ref, owners_ref, facts_ref):
    count, frames = owners_ref.shape
    taps = facts_ref.shape[1]
    me = lax.axis_index("seq")
    owners = owners_ref[...]
    ranks = ranks_of(owners, count)
    position = iota((count, frames), 0) * frames + iota((count, frames), 1)
    relative = jnp.bitwise_xor(owners.astype(jnp.int32), me)
    relative = (relative >> 1) + (relative & 1) * (count // 2)
    rows_of = [relative.astype(F32), ranks]
    for tap in range(1, taps):
        later = position + tap
        valid = (later < count * frames) & (position >= start_below(later, lengths_ref))
        rows_of.append(valid.astype(F32))
    eye = (iota((frames, frames), 0) == iota((frames, frames), 1)).astype(BF16)
    owner, rank, *valid = [
        lax.dot_general(
            eye, lines.astype(BF16), (((1,), (1,)), ((), ())), preferred_element_type=F32
        )
        for lines in rows_of
    ]
    lane = iota((frames, taps), 1)
    for block in range(count):
        here = slice(block, block + 1)
        facts = owner[:, here] * rows + (rank[:, here] + block * capacity)
        for tap in range(1, taps):
            facts = jnp.where(lane == tap, valid[tap - 1][:, here], facts)
        facts_ref[block * frames : (block + 1) * frames, :] = facts.astype(jnp.int32)


def spread_kernel(count, frames, taps, *refs):
    backs = refs[: count // 2 + 1]
    lines_ref, facts_ref, send_ref, windows_ref, gain_ref, gathered, wide = refs[len(backs) :]
    rows, latent_width = backs[0].shape
    share = lines_ref.shape[0] // 2
    gain_rows = gain_ref.shape[0]
    gain = jnp.zeros((gain_rows, latent_width), F32)
    for far, back_ref in enumerate(backs[:-1]):
        gathered[far * rows : (far + 1) * rows, :] = back_ref[...]
    far_count = count // 2
    gathered[far_count * rows :, :] = backs[-1][...]
    for rel in range(count):
        gain = gain + gathered[rel * rows : (rel + 1) * rows, :].astype(F32)[rows - gain_rows :]
    gain_ref[...] = gain
    for block in range(count):
        here = slice(block * frames, (block + 1) * frames)
        placed = iota((frames, count * rows), 1) == facts_ref[here, 0:1]
        wide[here, :] = jnp.dot(
            placed.astype(F32).astype(BF16), gathered[...], preferred_element_type=F32
        )
    wide[count * frames :, :] = jnp.zeros((8, latent_width), F32)
    for block in range(count):
        here = slice(block * frames, (block + 1) * frames)
        windows_ref[here, 0:latent_width] = wide[here, :].astype(BF16)
        for tap in range(1, taps):
            later = wide[block * frames + tap : (block + 1) * frames + tap, :]
            later = jnp.where(facts_ref[here, tap : tap + 1] > 0, later, 0.0)
            windows_ref[here, tap * latent_width : (tap + 1) * latent_width] = later.astype(BF16)
    part = jnp.dot(lines_ref[...], windows_ref[...], preferred_element_type=F32)
    for y in (0, 1):
        for tap in range(taps):
            at = (y * taps + tap) * share
            send_ref[at : at + share, :] = part[
                y * share : (y + 1) * share, tap * latent_width : (tap + 1) * latent_width
            ].astype(BF16)
    high = gain.astype(BF16)
    at = 2 * taps * share
    send_ref[at : at + 2 * gain_rows, :] = jnp.concatenate(
        [high.astype(F32), gain - high.astype(F32)], axis=0
    ).astype(BF16)


def channel_kernel(orders, *refs):
    turned_refs, out_refs = refs[: len(orders)], refs[len(orders) :]
    seq, book = lax.axis_index("seq"), lax.axis_index("book")
    share = turned_refs[0].shape[1] // 4
    for turned_ref, order in zip(turned_refs, orders):
        frames = turned_ref.shape[2]
        for index, rel in enumerate(order):
            lanes = pl.ds(pl.multiple_of(jnp.bitwise_xor(seq, rel) * frames, frames), frames)
            for core, out_ref in enumerate(out_refs):
                for y in (0, 1):
                    at = jnp.bitwise_xor(book, 2 * y + core) * share
                    out_ref[y * share : (y + 1) * share, lanes] = turned_ref[
                        index, pl.ds(pl.multiple_of(at, share), share), :
                    ]


def own_part_kernel(taps, lines_ref, windows_ref, out_ref):
    share, latent_width = lines_ref.shape[0] // 2, out_ref.shape[1]
    part = jnp.dot(lines_ref[...], windows_ref[...], preferred_element_type=F32)
    for y in (0, 1):
        for tap in range(taps):
            at = (y * taps + tap) * share
            out_ref[at : at + share, :] = part[
                y * share : (y + 1) * share, tap * latent_width : (tap + 1) * latent_width
            ]


def fold_kernel(kept_ref, got_ref, gain_ref, send_ref, mine_ref, gain_out_ref):
    half, gain_rows = mine_ref.shape[0], gain_ref.shape[0]
    mine_ref[...] = kept_ref[0:half, :] + got_ref[0:half, :].astype(F32)
    send_ref[0:half, :] = (
        kept_ref[half : 2 * half, :] + got_ref[half : 2 * half, :].astype(F32)
    ).astype(BF16)
    pair = got_ref[2 * half : 2 * half + 2 * gain_rows, :].astype(F32)
    gain = gain_ref[...] + (pair[:gain_rows] + pair[gain_rows:])
    gain_out_ref[...] = gain
    high = gain.astype(BF16).astype(F32)
    send_ref[half : half + 2 * gain_rows, :] = jnp.concatenate(
        [high, gain - high], axis=0
    ).astype(BF16)


def finish_kernel(mine_ref, got_ref, gain_ref, out_ref, gain_out_ref):
    half, gain_rows = mine_ref.shape[0], gain_ref.shape[0]
    out_ref[...] = mine_ref[...] + got_ref[0:half, :].astype(F32)
    pair = got_ref[half : half + 2 * gain_rows, :].astype(F32)
    gain = gain_ref[...] + (pair[:gain_rows] + pair[gain_rows:])
    step = gain.shape[1]
    for line in range(gain_rows):
        gain_out_ref[:, line * step : (line + 1) * step] = gain[line : line + 1]


def feature_kernel(feat_ref, windows_ref, w_ref, out_ref):
    frames = feat_ref.shape[0]
    taps, _, latent_width = w_ref.shape
    at = pl.multiple_of(lax.axis_index("seq") * frames, frames)
    total = jnp.zeros(feat_ref.shape, F32)
    for tap in range(taps):
        window = windows_ref[
            pl.ds(at, frames), tap * latent_width : (tap + 1) * latent_width
        ]
        total = total + lax.dot_general(
            window, w_ref[tap], (((1,), (1,)), ((), ())), preferred_element_type=F32
        )
    feats = feat_ref[...].astype(F32)
    slope = jnp.where(feats > 0, 1.0, jnp.exp(jnp.minimum(feats, 0.0)))
    out_ref[...] = (slope * total).astype(BF16)


def call(kernel, outs, operands, scratch=(), smem=0, flops=0):
    return pl.pallas_call(
        kernel,
        out_shape=outs,
        in_specs=[SMEM] * smem + [VMEM] * (len(operands) - smem),
        out_specs=jax.tree.map(lambda _: VMEM, outs),
        scratch_shapes=list(scratch),
        compiler_params=pltpu.CompilerParams(vmem_limit_bytes=24 * 2**20),
        cost_estimate=pl.CostEstimate(flops=flops, bytes_accessed=1024, transcendentals=0),
    )(*operands)


def shape(dims, dtype=BF16):
    return jax.ShapeDtypeStruct(dims, dtype)


def per_device(features, lengths, owner, w_enc, w_in, gain, cotangent):
    feats = features[0]
    cot = cotangent[0]
    book_lengths = lengths[0]
    frames, channels = feats.shape
    taps, _, latent_width = w_enc.shape
    slots, width = cot.shape
    count = lax.axis_size("seq")
    far_count = count // 2
    fars = range(1, far_count)
    capacity = max(2, frames // count + 1)
    piece = round_up(capacity + 1, 16)
    gain_rows = width // latent_width
    rows = round_up(slots + gain_rows, 16)
    half = channels // 4

    columns = w_in.shape[1]
    padded, turned = call(
        activate_kernel,
        [shape((24 + frames, channels), F32), shape((channels, frames))],
        (feats,),
        flops=HEAVY // 10,
    )
    total, placed, edge, named = call(
        functools.partial(encode_kernel, piece),
        [
            shape((frames, latent_width), F32),
            shape((count * piece, frames)),
            shape((8, latent_width), F32),
            shape((1, latent_width), F32),
        ],
        (book_lengths, padded, owner[0].T, w_enc),
        smem=1,
    )
    w_own, edge, turned = lax.optimization_barrier((w_in.T, edge, turned))
    edge = shifted(edge, "seq", 1)
    w_far = [w_own] + [swap(w_own, "seq", 2 * far) for far in fars]
    held = jnp.stack([turned, swap(turned, "seq", 4)])
    sent = call(
        functools.partial(place_kernel, piece),
        [shape((2 * piece, latent_width))] * far_count,
        (total, edge, placed, named),
    )
    held, sent = lax.optimization_barrier((held, sent))
    landed = [sent[0]] + [swap(sent[far], "seq", 2 * far) for far in fars]
    w_far = after(w_far, landed[1], landed[2])
    (w_line,) = call(
        functools.partial(join_rows_kernel, 0),
        [shape((far_count * columns, latent_width))],
        tuple(w_far),
        flops=HEAVY,
    )
    w_near = swap(w_line, "seq", 1)
    w_side = swap(w_line, "book", 2)
    w_diag = swap(w_line, ("seq", "book"), 4 + 2)
    got = swap(held, "seq", 2)
    (near,) = call(
        functools.partial(join_rows_kernel, piece),
        [shape((far_count * piece, latent_width))],
        tuple(landed),
        flops=HEAVY,
    )
    near = swap(near, "seq", 1)
    w_chips = [w_line, w_near, w_side, w_diag]
    w_chips, got = lax.optimization_barrier((w_chips, got))
    held = jnp.concatenate([held, got])
    w_pieces = w_chips + [swap(block, "book", 1) for block in w_chips]
    second = swap(held, "seq", 1)
    turned_all = [held, second]
    orders = [[0, 4, 2, 6], [1, 5, 3, 7]]

    back, hidden_grad, arrived, owners = call(
        functools.partial(middle_kernel, piece, capacity, frames, count, columns),
        [
            shape((rows, latent_width)),
            shape((rows, width)),
            shape((rows, latent_width)),
            shape((count, frames), F32),
        ],
        (*landed, near, *w_pieces, gain[None], cot),
        scratch=[
            pltpu.VMEM((count * piece, latent_width), BF16),
            pltpu.VMEM((width, latent_width), BF16),
            pltpu.VMEM((slots, width), F32),
            pltpu.VMEM((rows, latent_width), F32),
        ],
        flops=HEAVY,
    )
    backs = [back] + [swap(back, "seq", 2 * far) for far in fars]
    (near_backs,) = call(
        functools.partial(join_rows_kernel, 0),
        [shape((far_count * rows, latent_width))],
        tuple(backs),
        flops=HEAVY,
    )
    near_backs = swap(near_backs, "seq", 1)

    (facts,) = call(
        functools.partial(prepare_kernel, capacity, rows),
        [shape((count * frames, taps), jnp.int32)],
        (book_lengths, owners),
        smem=1,
        flops=HEAVY,
    )
    w_send, w_keep = call(
        functools.partial(projection_kernel, count),
        [shape((2 * count, columns, latent_width))] * 2,
        (hidden_grad, arrived),
    )
    w_got, facts = lax.optimization_barrier((swap(w_send, "book", 1), facts))
    w_sum = w_keep.astype(F32) + w_got.astype(F32)
    w_parts = [w_sum[at : at + far_count].astype(BF16) for at in range(0, 2 * count, far_count)]
    w_sum = w_sum[:far_count] + swap(w_parts[1], "seq", 1).astype(F32)
    w_sum = w_sum + swap(w_parts[2], "book", 2).astype(F32)
    w_sum = w_sum + swap(w_parts[3], ("seq", "book"), 4 + 2).astype(F32)
    own_lines, sent_lines = call(
        functools.partial(channel_kernel, orders),
        [shape((2 * half, count * frames))] * 2,
        tuple(after(turned_all, *w_parts)),
        flops=HEAVY,
    )
    message = 2 * taps * half + 2 * gain_rows
    k_send, windows, gain_seq = call(
        functools.partial(spread_kernel, count, frames, taps),
        [
            shape((message, latent_width)),
            shape((count * frames, taps * latent_width)),
            shape((gain_rows, latent_width), F32),
        ],
        (*backs, near_backs, sent_lines, facts),
        scratch=[
            pltpu.VMEM((count * rows, latent_width), BF16),
            pltpu.VMEM((count * frames + 8, latent_width), F32),
        ],
        flops=HEAVY,
    )
    k_got = swap(k_send, "book", 1)
    (k_kept,) = call(
        functools.partial(own_part_kernel, taps),
        [shape((2 * taps * half, latent_width), F32)],
        (own_lines, windows),
        flops=HEAVY,
    )
    y_send, k_mine, gain_pair = call(
        fold_kernel,
        [
            shape((taps * half + 2 * gain_rows, latent_width)),
            shape((taps * half, latent_width), F32),
            shape((gain_rows, latent_width), F32),
        ],
        (k_kept, k_got, gain_seq),
    )
    y_got = swap(y_send, "book", 2)
    w_far = [w_sum[far].astype(BF16) for far in fars]
    w_far = [after(block, k_send) for block in w_far[:0]] + [after(block, y_send) for block in w_far[0:]]
    w_total = w_sum[0]
    for far in fars:
        w_total = w_total + swap(w_far[far - 1], "seq", 2 * far).astype(F32)
    (feature_grad,) = call(
        feature_kernel,
        [shape(feats.shape)],
        (feats, after(windows, y_send), w_enc),
        flops=HEAVY,
    )
    y_got = after(y_got, feature_grad)
    kernel_mine, gain_total = call(
        finish_kernel,
        [shape((taps * half, latent_width), F32), shape((1, width), F32)],
        (k_mine, y_got, gain_pair),
    )
    return (
        feature_grad[None],
        kernel_mine.reshape(taps, half, latent_width),
        w_total.T,
        gain_total[0],
    )


def fits(mesh):
    count = mesh.shape["seq"]
    return mesh.shape["book"] == 4 and count in (2, 4, 8)


def solution(mesh):
    placed = (
        P("book", "seq", None),
        P("book", None),
        P("book", "seq", None),
        P(),
        P(None, ("seq", "book")),
        P(),
        P("book", "seq", None),
    )
    return jax.shard_map(
        per_device if fits(mesh) else per_device_gather,
        mesh=mesh,
        in_specs=placed,
        out_specs=(P("book", "seq", None), P(None, "book", None), P(None, ("seq", "book")), P()),
        check_vma=False,
    )
```

```python
import functools

import jax
import jax.numpy as jnp
from jax import lax
from jax.experimental import pallas as pl
from jax.experimental.pallas import tpu as pltpu
from jax.sharding import PartitionSpec as P

F32 = jnp.float32
BF16 = jnp.bfloat16
HEAVY = 20000000000
VMEM = pl.BlockSpec(memory_space=pltpu.VMEM)
SMEM = pl.BlockSpec(memory_space=pltpu.SMEM)


def shifted(block, axis, distance):
    devices = range(lax.axis_size(axis))
    route = [(i - distance, i) for i in devices if i - distance in devices]
    return lax.ppermute(block, axis, route)


def book_mask(position, book_lengths, offset):
    starts = jnp.cumsum(book_lengths) - book_lengths
    start_of = jnp.max(jnp.where(starts[None, :] <= position[:, None], starts[None, :], 0), axis=1)
    return position - offset >= start_of


def per_device_gather(features, lengths, owner, w_enc, w_in, gain, cotangent):
    feature_rows = features[0]
    frames, channels = feature_rows.shape
    tap_count, _, latent_width = w_enc.shape
    seq_count = lax.axis_size("seq")
    book_count = lax.axis_size("book")
    capacity = max(2, frames // seq_count + 1)
    first_frame = lax.axis_index("seq") * frames
    position = first_frame + jnp.arange(frames + tap_count - 1, dtype=jnp.int32)
    tap_masks = [book_mask(position, lengths[0], offset) for offset in range(tap_count)]
    feats_wide = feature_rows.astype(jnp.float32)
    activated = jax.nn.elu(feats_wide).astype(jnp.bfloat16)
    left_edge = shifted(activated[frames - (tap_count - 1) :], "seq", 1)
    padded = jnp.concatenate([left_edge, activated], axis=0)
    tap_inputs = []
    for offset in range(tap_count):
        begin = tap_count - 1 - offset
        window = padded[begin : begin + frames]
        tap_inputs.append(
            jnp.where(tap_masks[offset][:frames, None], window, jnp.zeros_like(window))
        )
    stacked = jnp.concatenate(tap_inputs, axis=1)
    latent = jnp.dot(
        stacked,
        w_enc.reshape(tap_count * channels, latent_width),
        preferred_element_type=jnp.float32,
    ).astype(jnp.bfloat16)
    owner_rank = owner[0, :, 0]
    one_hot = (owner_rank[:, None] == jnp.arange(seq_count, dtype=jnp.int32)[None, :]).astype(
        jnp.int32
    )
    slot_rank = jnp.sum((jnp.cumsum(one_hot, axis=0) - one_hot) * one_hot, axis=1)
    slot_index = owner_rank * capacity + slot_rank
    placement = (
        slot_index[:, None] == jnp.arange(seq_count * capacity, dtype=jnp.int32)[None, :]
    ).astype(jnp.bfloat16)
    outgoing = lax.dot_general(
        placement, latent, (((0,), (0,)), ((), ())), preferred_element_type=jnp.float32
    ).astype(jnp.bfloat16)
    arrived = lax.all_to_all(
        outgoing.reshape(seq_count, capacity, latent_width),
        "seq",
        split_axis=0,
        concat_axis=0,
        tiled=True,
    )
    arrived = arrived.reshape(seq_count * capacity, latent_width)
    w_full = lax.all_gather(w_in, ("seq", "book"), axis=1, tiled=True)
    grad_out = cotangent[0].astype(jnp.float32)
    hidden = jnp.dot(arrived, w_full, preferred_element_type=jnp.float32)
    inv_rms = lax.rsqrt(jnp.mean(hidden * hidden, axis=1, keepdims=True) + 1e-05)
    normed = hidden * inv_rms
    gain_term = grad_out * gain[None, :]
    hidden_grad = (
        inv_rms * (gain_term - normed * jnp.mean(gain_term * normed, axis=1, keepdims=True))
    ).astype(jnp.bfloat16)
    latent_back = lax.dot_general(
        hidden_grad, w_full, (((1,), (1,)), ((), ())), preferred_element_type=jnp.float32
    ).astype(jnp.bfloat16)
    w_part = lax.dot_general(
        arrived, hidden_grad, (((0,), (0,)), ((), ())), preferred_element_type=jnp.float32
    )
    gain_part = jnp.sum(grad_out * normed, axis=0)
    returned = lax.all_to_all(
        latent_back.reshape(seq_count, capacity, latent_width),
        "seq",
        split_axis=0,
        concat_axis=0,
        tiled=True,
    )
    returned = returned.reshape(seq_count * capacity, latent_width)
    latent_grad = jnp.dot(placement, returned, preferred_element_type=jnp.float32).astype(
        jnp.bfloat16
    )
    right_edge = shifted(latent_grad[: tap_count - 1], "seq", -1)
    extended = jnp.concatenate([latent_grad, right_edge], axis=0)
    tap_grads = []
    for offset in range(tap_count):
        window = extended[offset : offset + frames]
        tap_grads.append(
            jnp.where(
                tap_masks[offset][offset : offset + frames, None], window, jnp.zeros_like(window)
            )
        )
    kernel_back = jnp.transpose(w_enc, (0, 2, 1)).reshape(tap_count * latent_width, channels)
    activ_grad = jnp.dot(
        jnp.concatenate(tap_grads, axis=1), kernel_back, preferred_element_type=jnp.float32
    )
    slope = jnp.where(feats_wide > 0, 1.0, jnp.exp(feats_wide))
    feature_grad = (slope * activ_grad).astype(jnp.bfloat16)
    kernel_part = lax.dot_general(
        stacked, latent_grad, (((0,), (0,)), ((), ())), preferred_element_type=jnp.float32
    )
    kernel_part = kernel_part.reshape(tap_count, channels, latent_width)
    kernel_total, gain_total = lax.psum((kernel_part, gain_part), ("seq", "book"))
    share_width = channels // book_count
    kernel_mine = lax.dynamic_slice_in_dim(
        kernel_total, lax.axis_index("book") * share_width, share_width, 1
    )
    columns = w_in.shape[1]
    split_grad = w_part.reshape(latent_width, seq_count, book_count * columns)
    split_grad = lax.psum_scatter(
        split_grad.astype(jnp.bfloat16), "book", scatter_dimension=2, tiled=True
    ).astype(jnp.float32)
    w_grad = lax.psum_scatter(split_grad, "seq", scatter_dimension=1, tiled=True).reshape(
        latent_width, columns
    )
    return (feature_grad[None], kernel_mine, w_grad, gain_total)


def round_up(value, unit):
    return -(-value // unit) * unit


def swap(block, axis, mask):
    return lax.ppermute(block, axis, [(i, i ^ mask) for i in range(lax.axis_size(axis))])


def after(block, *others):
    return lax.optimization_barrier((block, *others))[0]


def iota(shape, dim):
    return lax.broadcasted_iota(jnp.int32, shape, dim)


def elu_wide(x):
    low = jnp.minimum(x, 0.0)
    series = 1.0 + low / 6.0
    for order in (5.0, 4.0, 3.0, 2.0):
        series = 1.0 + (low / order) * series
    below = jnp.where(low > -0.25, low * series, jnp.exp(low) - 1.0)
    return jnp.where(x > 0, x, below)


def start_below(position, lengths_ref):
    best = jnp.zeros_like(position)
    start = jnp.int32(0)
    for book in range(lengths_ref.shape[0]):
        best = jnp.where(start <= position, jnp.maximum(best, start), best)
        start = start + lengths_ref[book]
    return best


def ranks_of(owner_rows, seq_count):
    blocks, frames = owner_rows.shape
    parts = [
        (iota((seq_count, frames), 0) == owner_rows[b : b + 1].astype(jnp.int32)).astype(F32)
        for b in range(blocks)
    ]
    named = jnp.concatenate(parts, axis=0)
    before = (iota((frames, frames), 0) < iota((frames, frames), 1)).astype(BF16)
    counted = jnp.dot(named.astype(BF16), before, preferred_element_type=F32) * named
    return jnp.concatenate(
        [
            jnp.sum(counted[b * seq_count : (b + 1) * seq_count], axis=0, keepdims=True)
            for b in range(blocks)
        ],
        axis=0,
    )


def activate_kernel(feat_ref, padded_ref, turned_ref):
    frames, channels = feat_ref.shape
    act = elu_wide(feat_ref[...].astype(F32)).astype(BF16).astype(F32)
    padded_ref[0:8, :] = jnp.zeros((8, channels), F32)
    padded_ref[8 : 8 + frames, :] = act
    padded_ref[8 + frames :, :] = jnp.zeros((16, channels), F32)
    turned_ref[...] = act.T.astype(BF16)


def collect_kernel(plan, *refs):
    out_ref, at = refs[-1], 0
    for index, start, rows in plan:
        out_ref[at : at + rows, :] = refs[index][start : start + rows, :]
        at += rows


def encode_kernel(piece, lengths_ref, padded, owner_ref, w_ref, out_ref, extra):
    frames, latent_width = owner_ref.shape[1], out_ref.shape[1]
    taps = w_ref.shape[0]
    edges = taps - 1
    me = lax.axis_index("seq")
    seq_count = out_ref.shape[0] // piece
    owner = owner_ref[...]
    rank = ranks_of(owner, seq_count).astype(jnp.int32)
    row = jnp.bitwise_xor(owner, me) * piece + rank
    placed = (iota((seq_count * piece, frames), 0) == row).astype(F32).astype(BF16)
    position = me * frames + iota((frames, 1), 0)
    start_of = start_below(position, lengths_ref)
    beyond = (me + 1) * frames + iota((16, 1), 0)
    start_beyond = start_below(beyond, lengths_ref)
    total = jnp.zeros((frames, latent_width), F32)
    edge = jnp.zeros((16, latent_width), F32)
    for tap in range(taps):
        window = padded[8 - tap : 8 - tap + frames, :]
        window = jnp.where(position - tap >= start_of, window, 0.0).astype(BF16)
        total = total + jnp.dot(window, w_ref[tap], preferred_element_type=F32)
        if tap:
            window = padded[8 + frames - tap : 24 + frames - tap, :]
            window = jnp.where(beyond - tap >= start_beyond, window, 0.0).astype(BF16)
            edge = edge + jnp.dot(window, w_ref[tap], preferred_element_type=F32)
    latent = total.astype(BF16)
    outgoing = jnp.dot(placed, latent, preferred_element_type=F32)
    first, edge = total[:edges], edge[:edges]
    high = edge.astype(BF16).astype(F32)
    extra[...] = jnp.zeros_like(extra)
    at = piece - 1 - 3 * edges
    extra[at : at + edges, :] = first - latent[:8].astype(F32)[:edges]
    extra[at + edges : at + 2 * edges, :] = high
    extra[at + 2 * edges : at + 3 * edges, :] = edge - high
    extra[piece - 1 : piece, 0:frames] = owner.astype(F32)
    for rel in range(seq_count):
        here = slice(rel * piece, (rel + 1) * piece)
        out_ref[here, :] = (outgoing[here] + extra[...]).astype(BF16)


def join_rows_kernel(skip, *refs):
    rows = refs[0].shape[0] - skip
    for index, ref in enumerate(refs[:-1]):
        refs[-1][index * rows : (index + 1) * rows, :] = ref[skip:, :]


def middle_kernel(piece, capacity, frames, count, columns, edges, *refs):
    far_count = count // 2
    gathered, w_refs = refs[0], refs[1:9]
    gain_ref, cot_ref, back_ref, hg_ref, arrived_ref, owners_ref, w_full, hidden, back = refs[9:]
    slots, width = cot_ref.shape
    rows = back_ref.shape[0]
    latent_width = back_ref.shape[1]
    seq, book = lax.axis_index("seq"), lax.axis_index("book")
    for rel in range(count):
        line = gathered[rel * piece : (rel + 1) * piece, 0:frames].astype(F32)
        owners_ref[pl.ds(jnp.bitwise_xor(seq, rel), 1), :] = line[piece - 1 : piece, :]
    for index, w_ref in enumerate(w_refs):
        near_seq, near_y, near_core = index & 1, (index >> 1) & 1, index >> 2
        for far in range(far_count):
            at = jnp.bitwise_xor(seq, 2 * far + near_seq) * 4 + jnp.bitwise_xor(
                book, near_y * 2 + near_core
            )
            w_full[pl.ds(pl.multiple_of(at * columns, columns), columns), :] = w_ref[
                far * columns : (far + 1) * columns, :
            ]
    slot = iota((rows, 1), 0)
    source = jnp.zeros_like(slot)
    for block in range(1, count):
        source = source + (slot >= block * capacity).astype(jnp.int32)
    place = slot - source * capacity
    base = jnp.bitwise_xor(source, seq) * piece
    before = jnp.bitwise_xor(source - 1, seq) * piece
    column = iota((rows, count * piece), 1)
    picked = column == jnp.where(slot < slots, base + place, -1)
    taken = jnp.zeros_like(slot)
    at = piece - 1 - 3 * edges
    for edge in range(edges):
        owner = jnp.zeros((rows, 1), F32)
        for block in range(count):
            owner = jnp.where(source == block, owners_ref[block : block + 1, edge : edge + 1], owner)
        mine = (owner == seq.astype(F32)) & (slot < slots)
        here = mine & (place == taken)
        taken = taken + mine.astype(jnp.int32)
        rest = jnp.where(here, base + at + edge, -1)
        share = jnp.where(here & (source > 0), before + at + edges + edge, -1)
        share_rest = jnp.where(share >= 0, share + edges, -1)
        picked = picked | (column == rest) | (column == share) | (column == share_rest)
    picked = picked.astype(F32).astype(BF16)
    arrived = jnp.dot(picked, gathered[...], preferred_element_type=F32).astype(BF16)
    arrived_ref[...] = arrived
    step = latent_width
    squares = jnp.zeros((slots, step), F32)
    crossed = jnp.zeros((slots, step), F32)
    for at in range(0, width, step):
        part = lax.dot_general(
            arrived, w_full[at : at + step, :], (((1,), (1,)), ((), ())), preferred_element_type=F32
        )[:slots]
        hidden[:, at : at + step] = part
        squares = squares + part * part
        scaled = cot_ref[:, at : at + step].astype(F32) * gain_ref[:, at : at + step]
        crossed = crossed + part * scaled
    inv = lax.rsqrt(jnp.sum(squares, axis=1, keepdims=True) / width + 1e-05)
    pull = inv * inv * (jnp.sum(crossed, axis=1, keepdims=True) / width)
    total = jnp.zeros((rows, latent_width), F32)
    for at in range(0, width, step):
        part = hidden[:, at : at + step]
        grad_out = cot_ref[:, at : at + step].astype(F32)
        scaled = grad_out * gain_ref[:, at : at + step]
        grad = inv * (scaled - part * pull)
        grad = jnp.concatenate([grad, jnp.zeros((rows - slots, step), F32)], axis=0).astype(BF16)
        hg_ref[:, at : at + step] = grad
        total = total + jnp.dot(grad, w_full[at : at + step, :], preferred_element_type=F32)
        line = slots + at // step
        back[line : line + 1, :] = jnp.sum(grad_out * (part * inv), axis=0, keepdims=True)
    back[0:slots, :] = total[:slots]
    for line in range(slots + width // step, rows):
        back[line : line + 1, :] = jnp.zeros((1, latent_width), F32)
    back_ref[...] = back[...].astype(BF16)


def chip_order(count):
    return [(y, near, far) for y in (0, 1) for near in (0, 1) for far in range(count // 2)]


def projection_kernel(count, hg_ref, arrived_ref, send_ref, keep_ref):
    seq, book = lax.axis_index("seq"), lax.axis_index("book")
    core = jnp.bitwise_and(book, 1)
    chip = seq * 2 + (book >> 1)
    half = send_ref.shape[1]
    arrived = arrived_ref[...]
    for place, (y, near, far) in enumerate(chip_order(count)):
        at = jnp.bitwise_xor(chip, (2 * far + near) * 2 + y)
        grad = hg_ref[:, pl.ds(pl.multiple_of(at * 2 * half, 2 * half), 2 * half)]
        part = lax.dot_general(
            grad, arrived, (((0,), (0,)), ((), ())), preferred_element_type=F32
        )
        low, high = part[:half], part[half:]
        send_ref[place] = jnp.where(core == 0, high, low).astype(BF16)
        keep_ref[place] = jnp.where(core == 0, low, high).astype(BF16)


def prepare_kernel(capacity, rows, lengths_ref, owners_ref, facts_ref):
    count, frames = owners_ref.shape
    taps = facts_ref.shape[1]
    me = lax.axis_index("seq")
    owners = owners_ref[...]
    ranks = ranks_of(owners, count)
    position = iota((count, frames), 0) * frames + iota((count, frames), 1)
    relative = jnp.bitwise_xor(owners.astype(jnp.int32), me)
    relative = (relative >> 1) + (relative & 1) * (count // 2)
    rows_of = [relative.astype(F32), ranks]
    for tap in range(1, taps):
        later = position + tap
        valid = (later < count * frames) & (position >= start_below(later, lengths_ref))
        rows_of.append(valid.astype(F32))
    eye = (iota((frames, frames), 0) == iota((frames, frames), 1)).astype(BF16)
    owner, rank, *valid = [
        lax.dot_general(
            eye, lines.astype(BF16), (((1,), (1,)), ((), ())), preferred_element_type=F32
        )
        for lines in rows_of
    ]
    lane = iota((frames, taps), 1)
    for block in range(count):
        here = slice(block, block + 1)
        facts = owner[:, here] * rows + (rank[:, here] + block * capacity)
        for tap in range(1, taps):
            facts = jnp.where(lane == tap, valid[tap - 1][:, here], facts)
        facts_ref[block * frames : (block + 1) * frames, :] = facts.astype(jnp.int32)


def spread_kernel(count, frames, taps, *refs):
    backs = refs[: count // 2 + 2]
    lines_ref, facts_ref, send_ref, windows_ref, gain_ref, gathered, wide = refs[len(backs) :]
    rows, latent_width = backs[0].shape
    share = lines_ref.shape[0] // 2
    gain_rows = gain_ref.shape[0]
    gain = jnp.zeros((gain_rows, latent_width), F32)
    at = 0
    for back_ref in backs:
        gathered[at : at + back_ref.shape[0], :] = back_ref[...]
        at += back_ref.shape[0]
    for rel in range(count):
        gain = gain + gathered[rel * rows : (rel + 1) * rows, :].astype(F32)[rows - gain_rows :]
    gain_ref[...] = gain
    for block in range(count):
        here = slice(block * frames, (block + 1) * frames)
        placed = iota((frames, count * rows), 1) == facts_ref[here, 0:1]
        wide[here, :] = jnp.dot(
            placed.astype(F32).astype(BF16), gathered[...], preferred_element_type=F32
        )
    wide[count * frames :, :] = jnp.zeros((8, latent_width), F32)
    for block in range(count):
        here = slice(block * frames, (block + 1) * frames)
        windows_ref[here, 0:latent_width] = wide[here, :].astype(BF16)
        for tap in range(1, taps):
            later = wide[block * frames + tap : (block + 1) * frames + tap, :]
            later = jnp.where(facts_ref[here, tap : tap + 1] > 0, later, 0.0)
            windows_ref[here, tap * latent_width : (tap + 1) * latent_width] = later.astype(BF16)
    part = jnp.dot(lines_ref[...], windows_ref[...], preferred_element_type=F32)
    for y in (0, 1):
        for tap in range(taps):
            at = (y * taps + tap) * share
            send_ref[at : at + share, :] = part[
                y * share : (y + 1) * share, tap * latent_width : (tap + 1) * latent_width
            ].astype(BF16)
    high = gain.astype(BF16)
    at = 2 * taps * share
    send_ref[at : at + 2 * gain_rows, :] = jnp.concatenate(
        [high.astype(F32), gain - high.astype(F32)], axis=0
    ).astype(BF16)


def channel_kernel(orders, *refs):
    turned_refs, out_refs = refs[: len(orders)], refs[len(orders) :]
    seq, book = lax.axis_index("seq"), lax.axis_index("book")
    share = turned_refs[0].shape[1] // 4
    for turned_ref, order in zip(turned_refs, orders):
        frames = turned_ref.shape[2]
        for index, rel in enumerate(order):
            lanes = pl.ds(pl.multiple_of(jnp.bitwise_xor(seq, rel) * frames, frames), frames)
            for core, out_ref in enumerate(out_refs):
                for y in (0, 1):
                    at = jnp.bitwise_xor(book, 2 * y + core) * share
                    out_ref[y * share : (y + 1) * share, lanes] = turned_ref[
                        index, pl.ds(pl.multiple_of(at, share), share), :
                    ]


def own_part_kernel(taps, lines_ref, windows_ref, out_ref):
    share, latent_width = lines_ref.shape[0] // 2, out_ref.shape[1]
    part = jnp.dot(lines_ref[...], windows_ref[...], preferred_element_type=F32)
    for y in (0, 1):
        for tap in range(taps):
            at = (y * taps + tap) * share
            out_ref[at : at + share, :] = part[
                y * share : (y + 1) * share, tap * latent_width : (tap + 1) * latent_width
            ]


def fold_kernel(kept_ref, got_ref, gain_ref, send_ref, mine_ref, gain_out_ref):
    half, gain_rows = mine_ref.shape[0], gain_ref.shape[0]
    mine_ref[...] = kept_ref[0:half, :] + got_ref[0:half, :].astype(F32)
    send_ref[0:half, :] = (
        kept_ref[half : 2 * half, :] + got_ref[half : 2 * half, :].astype(F32)
    ).astype(BF16)
    pair = got_ref[2 * half : 2 * half + 2 * gain_rows, :].astype(F32)
    gain = gain_ref[...] + (pair[:gain_rows] + pair[gain_rows:])
    gain_out_ref[...] = gain
    high = gain.astype(BF16).astype(F32)
    send_ref[half : half + 2 * gain_rows, :] = jnp.concatenate(
        [high, gain - high], axis=0
    ).astype(BF16)


def finish_kernel(mine_ref, got_ref, gain_ref, out_ref, gain_out_ref):
    half, gain_rows = mine_ref.shape[0], gain_ref.shape[0]
    out_ref[...] = mine_ref[...] + got_ref[0:half, :].astype(F32)
    pair = got_ref[half : half + 2 * gain_rows, :].astype(F32)
    gain = gain_ref[...] + (pair[:gain_rows] + pair[gain_rows:])
    step = gain.shape[1]
    for line in range(gain_rows):
        gain_out_ref[:, line * step : (line + 1) * step] = gain[line : line + 1]


def feature_kernel(feat_ref, windows_ref, w_ref, out_ref):
    frames = feat_ref.shape[0]
    taps, _, latent_width = w_ref.shape
    at = pl.multiple_of(lax.axis_index("seq") * frames, frames)
    total = jnp.zeros(feat_ref.shape, F32)
    for tap in range(taps):
        window = windows_ref[
            pl.ds(at, frames), tap * latent_width : (tap + 1) * latent_width
        ]
        total = total + lax.dot_general(
            window, w_ref[tap], (((1,), (1,)), ((), ())), preferred_element_type=F32
        )
    feats = feat_ref[...].astype(F32)
    slope = jnp.where(feats > 0, 1.0, jnp.exp(jnp.minimum(feats, 0.0)))
    out_ref[...] = (slope * total).astype(BF16)


def call(kernel, outs, operands, scratch=(), smem=0, flops=0):
    return pl.pallas_call(
        kernel,
        out_shape=outs,
        in_specs=[SMEM] * smem + [VMEM] * (len(operands) - smem),
        out_specs=jax.tree.map(lambda _: VMEM, outs),
        scratch_shapes=list(scratch),
        compiler_params=pltpu.CompilerParams(vmem_limit_bytes=24 * 2**20),
        cost_estimate=pl.CostEstimate(flops=flops, bytes_accessed=1024, transcendentals=0),
    )(*operands)


def collect(blocks, flops=0):
    arrays, plan = [], []
    for array, start, rows in blocks:
        found = [i for i, known in enumerate(arrays) if known is array]
        if not found:
            arrays.append(array)
        plan.append((found[0] if found else len(arrays) - 1, start, rows))
    total = sum(rows for _, _, rows in plan)
    (out,) = call(
        functools.partial(collect_kernel, tuple(plan)),
        [shape((total, arrays[0].shape[1]), arrays[0].dtype)],
        tuple(arrays),
        flops=flops,
    )
    return out


def shape(dims, dtype=BF16):
    return jax.ShapeDtypeStruct(dims, dtype)


def per_device(features, lengths, owner, w_enc, w_in, gain, cotangent):
    feats = features[0]
    cot = cotangent[0]
    book_lengths = lengths[0]
    frames, channels = feats.shape
    taps, _, latent_width = w_enc.shape
    slots, width = cot.shape
    count = lax.axis_size("seq")
    far_count = count // 2
    fars = range(1, far_count)
    capacity = max(2, frames // count + 1)
    piece = round_up(capacity + 1 + 3 * (taps - 1), 16)
    gain_rows = width // latent_width
    rows = round_up(slots + gain_rows, 16)
    half = channels // 4

    columns = w_in.shape[1]
    padded, turned = call(
        activate_kernel,
        [shape((24 + frames, channels), F32), shape((channels, frames))],
        (feats,),
        flops=HEAVY // 10,
    )
    (sent,) = call(
        functools.partial(encode_kernel, piece),
        [shape((count * piece, latent_width))],
        (book_lengths, padded, owner[0].T, w_enc),
        scratch=[pltpu.VMEM((piece, latent_width), F32)],
        smem=1,
    )
    pieces = {0: {far: (sent, 2 * far * piece, 2 * piece) for far in range(far_count)}}
    w_blocks = {0: (w_in.T, 0, columns)}
    held, order, mask = turned[None], [0], far_count // 2
    w_got = None
    while mask:
        sources = sorted(pieces)
        owners = [far for far in range(far_count) if far in pieces[0] and far & mask]
        message = [w_blocks[far] for far in sources]
        message += [pieces[source][far] for source in sources for far in owners]
        w_got = swap(collect(message), "seq", 2 * mask)
        at = 0
        for source in sources:
            w_blocks[source ^ mask] = (w_got, at, columns)
            at += columns
        for source in sources:
            pieces[source ^ mask] = {}
            for far in owners:
                pieces[source ^ mask][far ^ mask] = (w_got, at, 2 * piece)
                at += 2 * piece
                del pieces[source][far]
        held = after(held, w_got)
        got = swap(held, "seq", 2 * mask)
        held = jnp.concatenate([held, got])
        order = order + [far ^ mask for far in order]
        mask //= 2
    fars_of_w = [w_blocks[far] for far in range(far_count)]
    near = [pieces[far][0] for far in range(far_count)]
    x_send = collect(fars_of_w + [(array, at + piece, piece) for array, at, _ in near])
    w_line = collect(fars_of_w, flops=HEAVY)
    x_got = swap(x_send, "seq", 1)
    w_side = swap(w_line, "book", 2)
    w_diag = swap(w_line, ("seq", "book"), 4 + 2)
    w_chips = [w_line, x_got, w_side, w_diag]
    w_pieces = w_chips + [swap(block, "book", 1) for block in w_chips]
    turned_all = [held, swap(held, "seq", 1)]
    orders = [[2 * far for far in order], [2 * far + 1 for far in order]]
    gathered = []
    for far, (array, at, _) in enumerate(near):
        gathered += [(array, at, piece), (x_got, far_count * columns + far * piece, piece)]
    gathered = collect(gathered)

    back, hidden_grad, arrived, owners = call(
        functools.partial(middle_kernel, piece, capacity, frames, count, columns, taps - 1),
        [
            shape((rows, latent_width)),
            shape((rows, width)),
            shape((rows, latent_width)),
            shape((count, frames), F32),
        ],
        (gathered, *w_pieces, gain[None], cot),
        scratch=[
            pltpu.VMEM((width, latent_width), BF16),
            pltpu.VMEM((slots, width), F32),
            pltpu.VMEM((rows, latent_width), F32),
        ],
        flops=HEAVY,
    )
    backs = [back] + [swap(back, "seq", 2 * far) for far in fars]
    half_far = far_count // 2
    near_backs = []
    for at in range(0, far_count, half_far):
        joined = collect([(block, 0, rows) for block in backs[at : at + half_far]], flops=HEAVY)
        near_backs.append(swap(joined, "seq", 1))

    (facts,) = call(
        functools.partial(prepare_kernel, capacity, rows),
        [shape((count * frames, taps), jnp.int32)],
        (book_lengths, owners),
        smem=1,
        flops=HEAVY,
    )
    w_send, w_keep = call(
        functools.partial(projection_kernel, count),
        [shape((2 * count, columns, latent_width))] * 2,
        (hidden_grad, arrived),
    )
    w_got, facts = lax.optimization_barrier((swap(w_send, "book", 1), facts))
    w_sum = w_keep.astype(F32) + w_got.astype(F32)
    w_parts = [w_sum[at : at + far_count].astype(BF16) for at in range(0, 2 * count, far_count)]
    w_x = swap(w_parts[1], "seq", 1)
    w_y = swap(w_parts[2], "book", 2)
    w_d = swap(w_parts[3], ("seq", "book"), 4 + 2)
    own_lines, sent_lines = call(
        functools.partial(channel_kernel, orders),
        [shape((2 * half, count * frames))] * 2,
        tuple(after(turned_all, *w_parts)),
        flops=HEAVY,
    )
    message = 2 * taps * half + 2 * gain_rows
    k_send, windows, gain_seq = call(
        functools.partial(spread_kernel, count, frames, taps),
        [
            shape((message, latent_width)),
            shape((count * frames, taps * latent_width)),
            shape((gain_rows, latent_width), F32),
        ],
        (*backs, *near_backs, sent_lines, facts),
        scratch=[
            pltpu.VMEM((count * rows, latent_width), BF16),
            pltpu.VMEM((count * frames + 8, latent_width), F32),
        ],
        flops=HEAVY,
    )
    k_got = swap(k_send, "book", 1)
    (k_kept,) = call(
        functools.partial(own_part_kernel, taps),
        [shape((2 * taps * half, latent_width), F32)],
        (own_lines, windows),
        flops=HEAVY,
    )
    y_send, k_mine, gain_pair = call(
        fold_kernel,
        [
            shape((taps * half + 2 * gain_rows, latent_width)),
            shape((taps * half, latent_width), F32),
            shape((gain_rows, latent_width), F32),
        ],
        (k_kept, k_got, gain_seq),
    )
    y_got = swap(y_send, "book", 2)
    w_x, w_y, w_d = after((w_x, w_y, w_d), y_send)
    w_sum = w_sum[:far_count] + w_x.astype(F32) + w_y.astype(F32) + w_d.astype(F32)
    w_far = [w_sum[far].astype(BF16) for far in fars]
    w_total = w_sum[0]
    w_got = [swap(block, "seq", 2 * far) for far, block in zip(fars, w_far)]
    (feature_grad,) = call(
        feature_kernel,
        [shape(feats.shape)],
        (feats, after(windows, y_send), w_enc),
        flops=HEAVY,
    )
    y_got = after(y_got, feature_grad)
    kernel_mine, gain_total = call(
        finish_kernel,
        [shape((taps * half, latent_width), F32), shape((1, width), F32)],
        (k_mine, y_got, gain_pair),
    )
    for block in after(w_got, kernel_mine):
        w_total = w_total + block.astype(F32)
    return (
        feature_grad[None],
        kernel_mine.reshape(taps, half, latent_width),
        w_total.T,
        gain_total[0],
    )


def fits(mesh):
    count = mesh.shape["seq"]
    return mesh.shape["book"] == 4 and count == 8


def solution(mesh):
    placed = (
        P("book", "seq", None),
        P("book", None),
        P("book", "seq", None),
        P(),
        P(None, ("seq", "book")),
        P(),
        P("book", "seq", None),
    )
    return jax.shard_map(
        per_device if fits(mesh) else per_device_gather,
        mesh=mesh,
        in_specs=placed,
        out_specs=(P("book", "seq", None), P(None, "book", None), P(None, ("seq", "book")), P()),
        check_vma=False,
    )
```

```python
import functools

import jax
import jax.numpy as jnp
from jax import lax
from jax.experimental import pallas as pl
from jax.experimental.pallas import tpu as pltpu
from jax.sharding import PartitionSpec as P

F32 = jnp.float32
BF16 = jnp.bfloat16
HEAVY = 20000000000
VMEM = pl.BlockSpec(memory_space=pltpu.VMEM)
SMEM = pl.BlockSpec(memory_space=pltpu.SMEM)


def shifted(block, axis, distance):
    devices = range(lax.axis_size(axis))
    route = [(i - distance, i) for i in devices if i - distance in devices]
    return lax.ppermute(block, axis, route)


def book_mask(position, book_lengths, offset):
    starts = jnp.cumsum(book_lengths) - book_lengths
    start_of = jnp.max(jnp.where(starts[None, :] <= position[:, None], starts[None, :], 0), axis=1)
    return position - offset >= start_of


def per_device_gather(features, lengths, owner, w_enc, w_in, gain, cotangent):
    feature_rows = features[0]
    frames, channels = feature_rows.shape
    tap_count, _, latent_width = w_enc.shape
    seq_count = lax.axis_size("seq")
    book_count = lax.axis_size("book")
    capacity = max(2, frames // seq_count + 1)
    first_frame = lax.axis_index("seq") * frames
    position = first_frame + jnp.arange(frames + tap_count - 1, dtype=jnp.int32)
    tap_masks = [book_mask(position, lengths[0], offset) for offset in range(tap_count)]
    feats_wide = feature_rows.astype(jnp.float32)
    activated = jax.nn.elu(feats_wide).astype(jnp.bfloat16)
    left_edge = shifted(activated[frames - (tap_count - 1) :], "seq", 1)
    padded = jnp.concatenate([left_edge, activated], axis=0)
    tap_inputs = []
    for offset in range(tap_count):
        begin = tap_count - 1 - offset
        window = padded[begin : begin + frames]
        tap_inputs.append(
            jnp.where(tap_masks[offset][:frames, None], window, jnp.zeros_like(window))
        )
    stacked = jnp.concatenate(tap_inputs, axis=1)
    latent = jnp.dot(
        stacked,
        w_enc.reshape(tap_count * channels, latent_width),
        preferred_element_type=jnp.float32,
    ).astype(jnp.bfloat16)
    owner_rank = owner[0, :, 0]
    one_hot = (owner_rank[:, None] == jnp.arange(seq_count, dtype=jnp.int32)[None, :]).astype(
        jnp.int32
    )
    slot_rank = jnp.sum((jnp.cumsum(one_hot, axis=0) - one_hot) * one_hot, axis=1)
    slot_index = owner_rank * capacity + slot_rank
    placement = (
        slot_index[:, None] == jnp.arange(seq_count * capacity, dtype=jnp.int32)[None, :]
    ).astype(jnp.bfloat16)
    outgoing = lax.dot_general(
        placement, latent, (((0,), (0,)), ((), ())), preferred_element_type=jnp.float32
    ).astype(jnp.bfloat16)
    arrived = lax.all_to_all(
        outgoing.reshape(seq_count, capacity, latent_width),
        "seq",
        split_axis=0,
        concat_axis=0,
        tiled=True,
    )
    arrived = arrived.reshape(seq_count * capacity, latent_width)
    w_full = lax.all_gather(w_in, ("seq", "book"), axis=1, tiled=True)
    grad_out = cotangent[0].astype(jnp.float32)
    hidden = jnp.dot(arrived, w_full, preferred_element_type=jnp.float32)
    inv_rms = lax.rsqrt(jnp.mean(hidden * hidden, axis=1, keepdims=True) + 1e-05)
    normed = hidden * inv_rms
    gain_term = grad_out * gain[None, :]
    hidden_grad = (
        inv_rms * (gain_term - normed * jnp.mean(gain_term * normed, axis=1, keepdims=True))
    ).astype(jnp.bfloat16)
    latent_back = lax.dot_general(
        hidden_grad, w_full, (((1,), (1,)), ((), ())), preferred_element_type=jnp.float32
    ).astype(jnp.bfloat16)
    w_part = lax.dot_general(
        arrived, hidden_grad, (((0,), (0,)), ((), ())), preferred_element_type=jnp.float32
    )
    gain_part = jnp.sum(grad_out * normed, axis=0)
    returned = lax.all_to_all(
        latent_back.reshape(seq_count, capacity, latent_width),
        "seq",
        split_axis=0,
        concat_axis=0,
        tiled=True,
    )
    returned = returned.reshape(seq_count * capacity, latent_width)
    latent_grad = jnp.dot(placement, returned, preferred_element_type=jnp.float32).astype(
        jnp.bfloat16
    )
    right_edge = shifted(latent_grad[: tap_count - 1], "seq", -1)
    extended = jnp.concatenate([latent_grad, right_edge], axis=0)
    tap_grads = []
    for offset in range(tap_count):
        window = extended[offset : offset + frames]
        tap_grads.append(
            jnp.where(
                tap_masks[offset][offset : offset + frames, None], window, jnp.zeros_like(window)
            )
        )
    kernel_back = jnp.transpose(w_enc, (0, 2, 1)).reshape(tap_count * latent_width, channels)
    activ_grad = jnp.dot(
        jnp.concatenate(tap_grads, axis=1), kernel_back, preferred_element_type=jnp.float32
    )
    slope = jnp.where(feats_wide > 0, 1.0, jnp.exp(feats_wide))
    feature_grad = (slope * activ_grad).astype(jnp.bfloat16)
    kernel_part = lax.dot_general(
        stacked, latent_grad, (((0,), (0,)), ((), ())), preferred_element_type=jnp.float32
    )
    kernel_part = kernel_part.reshape(tap_count, channels, latent_width)
    kernel_total, gain_total = lax.psum((kernel_part, gain_part), ("seq", "book"))
    share_width = channels // book_count
    kernel_mine = lax.dynamic_slice_in_dim(
        kernel_total, lax.axis_index("book") * share_width, share_width, 1
    )
    columns = w_in.shape[1]
    split_grad = w_part.reshape(latent_width, seq_count, book_count * columns)
    split_grad = lax.psum_scatter(
        split_grad.astype(jnp.bfloat16), "book", scatter_dimension=2, tiled=True
    ).astype(jnp.float32)
    w_grad = lax.psum_scatter(split_grad, "seq", scatter_dimension=1, tiled=True).reshape(
        latent_width, columns
    )
    return (feature_grad[None], kernel_mine, w_grad, gain_total)


def round_up(value, unit):
    return -(-value // unit) * unit


def swap(block, axis, mask):
    return lax.ppermute(block, axis, [(i, i ^ mask) for i in range(lax.axis_size(axis))])


def after(block, *others):
    return lax.optimization_barrier((block, *others))[0]


def iota(shape, dim):
    return lax.broadcasted_iota(jnp.int32, shape, dim)


def elu_wide(x):
    low = jnp.minimum(x, 0.0)
    series = 1.0 + low / 6.0
    for order in (5.0, 4.0, 3.0, 2.0):
        series = 1.0 + (low / order) * series
    below = jnp.where(low > -0.25, low * series, jnp.exp(low) - 1.0)
    return jnp.where(x > 0, x, below)


def start_below(position, lengths_ref):
    best = jnp.zeros_like(position)
    start = jnp.int32(0)
    for book in range(lengths_ref.shape[0]):
        best = jnp.where(start <= position, jnp.maximum(best, start), best)
        start = start + lengths_ref[book]
    return best


def ranks_of(owner_rows, seq_count):
    blocks, frames = owner_rows.shape
    parts = [
        (iota((seq_count, frames), 0) == owner_rows[b : b + 1].astype(jnp.int32)).astype(F32)
        for b in range(blocks)
    ]
    named = jnp.concatenate(parts, axis=0)
    before = (iota((frames, frames), 0) < iota((frames, frames), 1)).astype(BF16)
    counted = jnp.dot(named.astype(BF16), before, preferred_element_type=F32) * named
    return jnp.concatenate(
        [
            jnp.sum(counted[b * seq_count : (b + 1) * seq_count], axis=0, keepdims=True)
            for b in range(blocks)
        ],
        axis=0,
    )


def activate_kernel(feat_ref, padded_ref, turned_ref):
    frames, channels = feat_ref.shape
    act = elu_wide(feat_ref[...].astype(F32)).astype(BF16).astype(F32)
    padded_ref[0:8, :] = jnp.zeros((8, channels), F32)
    padded_ref[8 : 8 + frames, :] = act
    padded_ref[8 + frames :, :] = jnp.zeros((16, channels), F32)
    turned_ref[...] = act.T.astype(BF16)


def collect_kernel(plan, *refs):
    out_ref, at = refs[-1], 0
    for index, start, rows in plan:
        out_ref[at : at + rows, :] = refs[index][start : start + rows, :]
        at += rows


def encode_kernel(piece, lengths_ref, padded, owner_ref, w_ref, out_ref, extra):
    frames, latent_width = owner_ref.shape[1], out_ref.shape[1]
    taps = w_ref.shape[0]
    edges = taps - 1
    me = lax.axis_index("seq")
    seq_count = out_ref.shape[0] // piece
    owner = owner_ref[...]
    rank = ranks_of(owner, seq_count).astype(jnp.int32)
    row = jnp.bitwise_xor(owner, me) * piece + rank
    placed = (iota((seq_count * piece, frames), 0) == row).astype(F32).astype(BF16)
    position = me * frames + iota((frames, 1), 0)
    start_of = start_below(position, lengths_ref)
    beyond = (me + 1) * frames + iota((16, 1), 0)
    start_beyond = start_below(beyond, lengths_ref)
    total = jnp.zeros((frames, latent_width), F32)
    edge = jnp.zeros((16, latent_width), F32)
    for tap in range(taps):
        window = padded[8 - tap : 8 - tap + frames, :]
        window = jnp.where(position - tap >= start_of, window, 0.0).astype(BF16)
        total = total + jnp.dot(window, w_ref[tap], preferred_element_type=F32)
        if tap:
            window = padded[8 + frames - tap : 24 + frames - tap, :]
            window = jnp.where(beyond - tap >= start_beyond, window, 0.0).astype(BF16)
            edge = edge + jnp.dot(window, w_ref[tap], preferred_element_type=F32)
    latent = total.astype(BF16)
    outgoing = jnp.dot(placed, latent, preferred_element_type=F32)
    first, edge = total[:edges], edge[:edges]
    high = edge.astype(BF16).astype(F32)
    extra[...] = jnp.zeros_like(extra)
    at = piece - 1 - 3 * edges
    extra[at : at + edges, :] = first - latent[:8].astype(F32)[:edges]
    extra[at + edges : at + 2 * edges, :] = high
    extra[at + 2 * edges : at + 3 * edges, :] = edge - high
    extra[piece - 1 : piece, 0:frames] = owner.astype(F32)
    for rel in range(seq_count):
        here = slice(rel * piece, (rel + 1) * piece)
        out_ref[here, :] = (outgoing[here] + extra[...]).astype(BF16)


def join_rows_kernel(skip, *refs):
    rows = refs[0].shape[0] - skip
    for index, ref in enumerate(refs[:-1]):
        refs[-1][index * rows : (index + 1) * rows, :] = ref[skip:, :]


def middle_kernel(piece, capacity, frames, count, columns, edges, *refs):
    far_count = count // 2
    gathered, w_refs = refs[0], refs[1:9]
    gain_ref, cot_ref, back_ref, hg_ref, arrived_ref, owners_ref, w_full, hidden, back = refs[9:]
    slots, width = cot_ref.shape
    rows = back_ref.shape[0]
    latent_width = back_ref.shape[1]
    seq, book = lax.axis_index("seq"), lax.axis_index("book")
    for rel in range(count):
        line = gathered[rel * piece : (rel + 1) * piece, 0:frames].astype(F32)
        owners_ref[pl.ds(jnp.bitwise_xor(seq, rel), 1), :] = line[piece - 1 : piece, :]
    for index, w_ref in enumerate(w_refs):
        near_seq, near_y, near_core = index & 1, (index >> 1) & 1, index >> 2
        for far in range(far_count):
            at = jnp.bitwise_xor(seq, 2 * far + near_seq) * 4 + jnp.bitwise_xor(
                book, near_y * 2 + near_core
            )
            w_full[pl.ds(pl.multiple_of(at * columns, columns), columns), :] = w_ref[
                far * columns : (far + 1) * columns, :
            ]
    slot = iota((rows, 1), 0)
    source = jnp.zeros_like(slot)
    for block in range(1, count):
        source = source + (slot >= block * capacity).astype(jnp.int32)
    place = slot - source * capacity
    base = jnp.bitwise_xor(source, seq) * piece
    before = jnp.bitwise_xor(source - 1, seq) * piece
    column = iota((rows, count * piece), 1)
    picked = column == jnp.where(slot < slots, base + place, -1)
    taken = jnp.zeros_like(slot)
    at = piece - 1 - 3 * edges
    for edge in range(edges):
        owner = jnp.zeros((rows, 1), F32)
        for block in range(count):
            owner = jnp.where(source == block, owners_ref[block : block + 1, edge : edge + 1], owner)
        mine = (owner == seq.astype(F32)) & (slot < slots)
        here = mine & (place == taken)
        taken = taken + mine.astype(jnp.int32)
        rest = jnp.where(here, base + at + edge, -1)
        share = jnp.where(here & (source > 0), before + at + edges + edge, -1)
        share_rest = jnp.where(share >= 0, share + edges, -1)
        picked = picked | (column == rest) | (column == share) | (column == share_rest)
    picked = picked.astype(F32).astype(BF16)
    arrived = jnp.dot(picked, gathered[...], preferred_element_type=F32).astype(BF16)
    arrived_ref[...] = arrived
    step = latent_width
    squares = jnp.zeros((slots, step), F32)
    crossed = jnp.zeros((slots, step), F32)
    for at in range(0, width, step):
        part = lax.dot_general(
            arrived, w_full[at : at + step, :], (((1,), (1,)), ((), ())), preferred_element_type=F32
        )[:slots]
        hidden[:, at : at + step] = part
        squares = squares + part * part
        scaled = cot_ref[:, at : at + step].astype(F32) * gain_ref[:, at : at + step]
        crossed = crossed + part * scaled
    inv = lax.rsqrt(jnp.sum(squares, axis=1, keepdims=True) / width + 1e-05)
    pull = inv * inv * (jnp.sum(crossed, axis=1, keepdims=True) / width)
    total = jnp.zeros((rows, latent_width), F32)
    for at in range(0, width, step):
        part = hidden[:, at : at + step]
        grad_out = cot_ref[:, at : at + step].astype(F32)
        scaled = grad_out * gain_ref[:, at : at + step]
        grad = inv * (scaled - part * pull)
        grad = jnp.concatenate([grad, jnp.zeros((rows - slots, step), F32)], axis=0).astype(BF16)
        hg_ref[:, at : at + step] = grad
        total = total + jnp.dot(grad, w_full[at : at + step, :], preferred_element_type=F32)
        line = slots + at // step
        back[line : line + 1, :] = jnp.sum(grad_out * (part * inv), axis=0, keepdims=True)
    back[0:slots, :] = total[:slots]
    for line in range(slots + width // step, rows):
        back[line : line + 1, :] = jnp.zeros((1, latent_width), F32)
    back_ref[...] = back[...].astype(BF16)


def chip_order(count):
    return [(y, near, far) for y in (0, 1) for near in (0, 1) for far in range(count // 2)]


def projection_kernel(count, hg_ref, arrived_ref, send_ref, keep_ref):
    seq, book = lax.axis_index("seq"), lax.axis_index("book")
    core = jnp.bitwise_and(book, 1)
    chip = seq * 2 + (book >> 1)
    half = send_ref.shape[1]
    arrived = arrived_ref[...]
    for place, (y, near, far) in enumerate(chip_order(count)):
        at = jnp.bitwise_xor(chip, (2 * far + near) * 2 + y)
        grad = hg_ref[:, pl.ds(pl.multiple_of(at * 2 * half, 2 * half), 2 * half)]
        part = lax.dot_general(
            grad, arrived, (((0,), (0,)), ((), ())), preferred_element_type=F32
        )
        low, high = part[:half], part[half:]
        send_ref[place] = jnp.where(core == 0, high, low).astype(BF16)
        keep_ref[place] = jnp.where(core == 0, low, high).astype(BF16)


def prepare_kernel(capacity, rows, lengths_ref, owners_ref, facts_ref):
    count, frames = owners_ref.shape
    taps = facts_ref.shape[1]
    me = lax.axis_index("seq")
    owners = owners_ref[...]
    ranks = ranks_of(owners, count)
    position = iota((count, frames), 0) * frames + iota((count, frames), 1)
    relative = jnp.bitwise_xor(owners.astype(jnp.int32), me)
    relative = jnp.where(relative & 1 == 1, -count, relative >> 1)
    rows_of = [relative.astype(F32), ranks]
    for tap in range(1, taps):
        later = position + tap
        valid = (later < count * frames) & (position >= start_below(later, lengths_ref))
        rows_of.append(valid.astype(F32))
    eye = (iota((frames, frames), 0) == iota((frames, frames), 1)).astype(BF16)
    owner, rank, *valid = [
        lax.dot_general(
            eye, lines.astype(BF16), (((1,), (1,)), ((), ())), preferred_element_type=F32
        )
        for lines in rows_of
    ]
    lane = iota((frames, taps), 1)
    for block in range(count):
        here = slice(block, block + 1)
        facts = owner[:, here] * rows + (rank[:, here] + block * capacity)
        for tap in range(1, taps):
            facts = jnp.where(lane == tap, valid[tap - 1][:, here], facts)
        facts_ref[block * frames : (block + 1) * frames, :] = facts.astype(jnp.int32)


def spread_kernel(count, frames, taps, *refs):
    backs = refs[: count // 2]
    lines_ref, facts_ref, send_ref, windows_ref, gain_ref, own_ref, peer_ref = refs[count // 2 : -2]
    gathered, wide = refs[-2:]
    rows, latent_width = backs[0].shape
    share = lines_ref.shape[0] // 2
    gain_rows = gain_ref.shape[0]
    gain = jnp.zeros((gain_rows, latent_width), F32)
    for far, back_ref in enumerate(backs):
        gathered[far * rows : (far + 1) * rows, :] = back_ref[...]
        gain = gain + back_ref[...].astype(F32)[rows - gain_rows :]
    gain_ref[...] = gain
    for block in range(count):
        here = slice(block * frames, (block + 1) * frames)
        placed = iota((frames, gathered.shape[0]), 1) == facts_ref[here, 0:1]
        wide[here, :] = jnp.dot(
            placed.astype(F32).astype(BF16), gathered[...], preferred_element_type=F32
        )
    wide[count * frames :, :] = jnp.zeros((16, latent_width), F32)
    me = lax.axis_index("seq")
    for out_ref, block in ((own_ref, me), (peer_ref, jnp.bitwise_xor(me, 1))):
        at = pl.multiple_of(block * frames, frames)
        out_ref[...] = wide[pl.ds(at, frames + 16), :].astype(BF16)
    for block in range(count):
        here = slice(block * frames, (block + 1) * frames)
        windows_ref[here, 0:latent_width] = wide[here, :].astype(BF16)
        for tap in range(1, taps):
            later = wide[block * frames + tap : (block + 1) * frames + tap, :]
            later = jnp.where(facts_ref[here, tap : tap + 1] > 0, later, 0.0)
            windows_ref[here, tap * latent_width : (tap + 1) * latent_width] = later.astype(BF16)
    part = jnp.dot(lines_ref[...], windows_ref[...], preferred_element_type=F32)
    for y in (0, 1):
        for tap in range(taps):
            at = (y * taps + tap) * share
            send_ref[at : at + share, :] = part[
                y * share : (y + 1) * share, tap * latent_width : (tap + 1) * latent_width
            ].astype(BF16)
    high = gain.astype(BF16)
    at = 2 * taps * share
    send_ref[at : at + 2 * gain_rows, :] = jnp.concatenate(
        [high.astype(F32), gain - high.astype(F32)], axis=0
    ).astype(BF16)


def channel_kernel(orders, *refs):
    turned_refs, out_refs = refs[: len(orders)], refs[len(orders) :]
    seq, book = lax.axis_index("seq"), lax.axis_index("book")
    share = turned_refs[0].shape[1] // 4
    for turned_ref, order in zip(turned_refs, orders):
        frames = turned_ref.shape[2]
        for index, rel in enumerate(order):
            lanes = pl.ds(pl.multiple_of(jnp.bitwise_xor(seq, rel) * frames, frames), frames)
            for core, out_ref in enumerate(out_refs):
                for y in (0, 1):
                    at = jnp.bitwise_xor(book, 2 * y + core) * share
                    out_ref[y * share : (y + 1) * share, lanes] = turned_ref[
                        index, pl.ds(pl.multiple_of(at, share), share), :
                    ]


def own_part_kernel(taps, lines_ref, windows_ref, out_ref):
    share, latent_width = lines_ref.shape[0] // 2, out_ref.shape[1]
    part = jnp.dot(lines_ref[...], windows_ref[...], preferred_element_type=F32)
    for y in (0, 1):
        for tap in range(taps):
            at = (y * taps + tap) * share
            out_ref[at : at + share, :] = part[
                y * share : (y + 1) * share, tap * latent_width : (tap + 1) * latent_width
            ]


def fold_kernel(kept_ref, got_ref, gain_ref, send_ref, mine_ref, gain_out_ref):
    half, gain_rows = mine_ref.shape[0], gain_ref.shape[0]
    mine_ref[...] = kept_ref[0:half, :] + got_ref[0:half, :].astype(F32)
    send_ref[0:half, :] = (
        kept_ref[half : 2 * half, :] + got_ref[half : 2 * half, :].astype(F32)
    ).astype(BF16)
    pair = got_ref[2 * half : 2 * half + 2 * gain_rows, :].astype(F32)
    gain = gain_ref[...] + (pair[:gain_rows] + pair[gain_rows:])
    gain_out_ref[...] = gain
    high = gain.astype(BF16).astype(F32)
    send_ref[half : half + 2 * gain_rows, :] = jnp.concatenate(
        [high, gain - high], axis=0
    ).astype(BF16)


def sum_kernel(mine_ref, got_ref, gain_ref, send_ref):
    half, gain_rows = mine_ref.shape[0], gain_ref.shape[0]
    send_ref[0:half, :] = (mine_ref[...] + got_ref[0:half, :].astype(F32)).astype(BF16)
    pair = got_ref[half : half + 2 * gain_rows, :].astype(F32)
    gain = gain_ref[...] + (pair[:gain_rows] + pair[gain_rows:])
    high = gain.astype(BF16).astype(F32)
    send_ref[half : half + 2 * gain_rows, :] = jnp.concatenate(
        [high, gain - high], axis=0
    ).astype(BF16)


def finish_kernel(mine_ref, got_ref, out_ref, gain_out_ref):
    half = out_ref.shape[0]
    gain_rows = (mine_ref.shape[0] - half) // 2
    out_ref[...] = mine_ref[0:half, :].astype(F32) + got_ref[0:half, :].astype(F32)
    gain = jnp.zeros((gain_rows, mine_ref.shape[1]), F32)
    for ref in (mine_ref, got_ref):
        pair = ref[half : half + 2 * gain_rows, :].astype(F32)
        gain = gain + (pair[:gain_rows] + pair[gain_rows:])
    step = gain.shape[1]
    for line in range(gain_rows):
        gain_out_ref[:, line * step : (line + 1) * step] = gain[line : line + 1]


def feature_kernel(feat_ref, own_ref, got_ref, facts_ref, w_ref, out_ref, wide):
    frames = feat_ref.shape[0]
    at = pl.multiple_of(lax.axis_index("seq") * frames, frames)
    wide[...] = own_ref[...].astype(F32) + got_ref[...].astype(F32)
    facts = facts_ref[pl.ds(at, frames), :]
    total = jnp.zeros(feat_ref.shape, F32)
    for tap in range(w_ref.shape[0]):
        window = wide[tap : tap + frames, :]
        if tap:
            window = jnp.where(facts[:, tap : tap + 1] > 0, window, 0.0)
        total = total + lax.dot_general(
            window.astype(BF16), w_ref[tap], (((1,), (1,)), ((), ())), preferred_element_type=F32
        )
    feats = feat_ref[...].astype(F32)
    slope = jnp.where(feats > 0, 1.0, jnp.exp(jnp.minimum(feats, 0.0)))
    out_ref[...] = (slope * total).astype(BF16)


def call(kernel, outs, operands, scratch=(), smem=0, flops=0):
    return pl.pallas_call(
        kernel,
        out_shape=outs,
        in_specs=[SMEM] * smem + [VMEM] * (len(operands) - smem),
        out_specs=jax.tree.map(lambda _: VMEM, outs),
        scratch_shapes=list(scratch),
        compiler_params=pltpu.CompilerParams(vmem_limit_bytes=24 * 2**20),
        cost_estimate=pl.CostEstimate(flops=flops, bytes_accessed=1024, transcendentals=0),
    )(*operands)


def collect(blocks, flops=0):
    arrays, plan = [], []
    for array, start, rows in blocks:
        found = [i for i, known in enumerate(arrays) if known is array]
        if not found:
            arrays.append(array)
        plan.append((found[0] if found else len(arrays) - 1, start, rows))
    total = sum(rows for _, _, rows in plan)
    (out,) = call(
        functools.partial(collect_kernel, tuple(plan)),
        [shape((total, arrays[0].shape[1]), arrays[0].dtype)],
        tuple(arrays),
        flops=flops,
    )
    return out


def shape(dims, dtype=BF16):
    return jax.ShapeDtypeStruct(dims, dtype)


def per_device(features, lengths, owner, w_enc, w_in, gain, cotangent):
    feats = features[0]
    cot = cotangent[0]
    book_lengths = lengths[0]
    frames, channels = feats.shape
    taps, _, latent_width = w_enc.shape
    slots, width = cot.shape
    count = lax.axis_size("seq")
    far_count = count // 2
    fars = range(1, far_count)
    capacity = max(2, frames // count + 1)
    piece = round_up(capacity + 1 + 3 * (taps - 1), 16)
    gain_rows = width // latent_width
    rows = round_up(slots + gain_rows, 16)
    half = channels // 4

    columns = w_in.shape[1]
    padded, turned = call(
        activate_kernel,
        [shape((24 + frames, channels), F32), shape((channels, frames))],
        (feats,),
        flops=HEAVY // 10,
    )
    (sent,) = call(
        functools.partial(encode_kernel, piece),
        [shape((count * piece, latent_width))],
        (book_lengths, padded, owner[0].T, w_enc),
        scratch=[pltpu.VMEM((piece, latent_width), F32)],
        smem=1,
    )
    pieces = {0: {far: (sent, 2 * far * piece, 2 * piece) for far in range(far_count)}}
    w_blocks = {0: (w_in.T, 0, columns)}
    held, mask = turned[None], far_count // 2
    w_got = None
    while mask:
        sources = sorted(pieces)
        owners = [far for far in range(far_count) if far in pieces[0] and far & mask]
        message = [w_blocks[far] for far in sources]
        message += [pieces[source][far] for source in sources for far in owners]
        w_got = swap(collect(message), "seq", 2 * mask)
        at = 0
        for source in sources:
            w_blocks[source ^ mask] = (w_got, at, columns)
            at += columns
        for source in sources:
            pieces[source ^ mask] = {}
            for far in owners:
                pieces[source ^ mask][far ^ mask] = (w_got, at, 2 * piece)
                at += 2 * piece
                del pieces[source][far]
        if mask == far_count // 2:
            joined = collect([w_blocks[far] for far in sorted(w_blocks)], flops=HEAVY)
            w_blocks = {far: (joined, i * columns, columns) for i, far in enumerate(sorted(w_blocks))}
        if mask < far_count // 2:
            held = after(held, w_got)
        got = swap(held, "seq", 2 * mask)
        if mask == far_count // 2:
            held = jnp.concatenate([held, got])
        mask //= 2
    x_first, x_last = swap(held, "seq", 1), swap(got, "seq", 1)
    fars_of_w = [w_blocks[far] for far in range(far_count)]
    near = [pieces[far][0] for far in range(far_count)]
    x_send = collect(fars_of_w + [(array, at + piece, piece) for array, at, _ in near])
    w_line = collect(fars_of_w)
    x_got = swap(x_send, "seq", 1)
    w_side = swap(w_line, "book", 2)
    w_diag = swap(w_line, ("seq", "book"), 4 + 2)
    w_chips = [w_line, x_got, w_side, w_diag]
    turned_all = [held, got, x_first, x_last]
    orders = [[0, 4], [2, 6], [1, 5], [3, 7]]
    gathered = []
    for far, (array, at, _) in enumerate(near):
        gathered += [(array, at, piece), (x_got, far_count * columns + far * piece, piece)]
    gathered = collect(gathered, flops=HEAVY)
    w_pieces = w_chips + [
        swap(after(block, gathered) if block is x_got else block, "book", 1) for block in w_chips
    ]

    back, hidden_grad, arrived, owners = call(
        functools.partial(middle_kernel, piece, capacity, frames, count, columns, taps - 1),
        [
            shape((rows, latent_width)),
            shape((rows, width)),
            shape((rows, latent_width)),
            shape((count, frames), F32),
        ],
        (gathered, *w_pieces, gain[None], cot),
        scratch=[
            pltpu.VMEM((width, latent_width), BF16),
            pltpu.VMEM((slots, width), F32),
            pltpu.VMEM((rows, latent_width), F32),
        ],
        flops=HEAVY,
    )
    backs = [back] + [swap(back, "seq", 2 * far) for far in fars]
    (facts,) = call(
        functools.partial(prepare_kernel, capacity, rows),
        [shape((count * frames, taps), jnp.int32)],
        (book_lengths, owners),
        smem=1,
        flops=HEAVY,
    )
    w_send, w_keep = call(
        functools.partial(projection_kernel, count),
        [shape((2 * count, columns, latent_width))] * 2,
        (hidden_grad, arrived),
    )
    w_got, facts = lax.optimization_barrier((swap(w_send, "book", 1), facts))
    w_sum = w_keep.astype(F32) + w_got.astype(F32)
    w_parts = [w_sum[at : at + far_count].astype(BF16) for at in range(0, 2 * count, far_count)]
    w_x = swap(w_parts[1], "seq", 1)
    w_y = swap(w_parts[2], "book", 2)
    w_d = swap(w_parts[3], ("seq", "book"), 4 + 2)
    own_lines, sent_lines = call(
        functools.partial(channel_kernel, orders),
        [shape((2 * half, count * frames))] * 2,
        tuple(after(turned_all, *w_parts)),
        flops=HEAVY,
    )
    message = 2 * taps * half + 2 * gain_rows
    k_send, windows, gain_seq, lines_own, lines_peer = call(
        functools.partial(spread_kernel, count, frames, taps),
        [
            shape((message, latent_width)),
            shape((count * frames, taps * latent_width)),
            shape((gain_rows, latent_width), F32),
            shape((frames + 16, latent_width)),
            shape((frames + 16, latent_width)),
        ],
        (*backs, sent_lines, facts),
        scratch=[
            pltpu.VMEM((far_count * rows, latent_width), BF16),
            pltpu.VMEM((count * frames + 16, latent_width), F32),
        ],
        flops=HEAVY,
    )
    k_got = swap(k_send, "book", 1)
    (k_kept,) = call(
        functools.partial(own_part_kernel, taps),
        [shape((2 * taps * half, latent_width), F32)],
        (own_lines, windows),
        flops=HEAVY,
    )
    y_send, k_mine, gain_pair = call(
        fold_kernel,
        [
            shape((taps * half + 2 * gain_rows, latent_width)),
            shape((taps * half, latent_width), F32),
            shape((gain_rows, latent_width), F32),
        ],
        (k_kept, k_got, gain_seq),
    )
    y_got = swap(y_send, "book", 2)
    lines_got = swap(after(lines_peer, y_send), "seq", 1)
    w_x, w_y, w_d = after((w_x, w_y, w_d), y_send)
    w_sum = w_sum[:far_count] + w_x.astype(F32) + w_y.astype(F32) + w_d.astype(F32)
    w_far = [w_sum[far].astype(BF16) for far in fars]
    w_total = w_sum[0]
    w_got = [swap(block, "seq", 2 * far) for far, block in zip(fars, w_far)]
    (x_send,) = call(
        sum_kernel,
        [shape((taps * half + 2 * gain_rows, latent_width))],
        (k_mine, y_got, gain_pair),
    )
    x_got = swap(x_send, "seq", 1)
    (feature_grad,) = call(
        feature_kernel,
        [shape(feats.shape)],
        (feats, lines_own, lines_got, facts, w_enc),
        scratch=[pltpu.VMEM((frames + 16, latent_width), F32)],
        flops=HEAVY,
    )
    x_got = after(x_got, feature_grad)
    kernel_mine, gain_total = call(
        finish_kernel,
        [shape((taps * half, latent_width), F32), shape((1, width), F32)],
        (x_send, x_got),
    )
    for block in after(w_got, kernel_mine):
        w_total = w_total + block.astype(F32)
    return (
        feature_grad[None],
        kernel_mine.reshape(taps, half, latent_width),
        w_total.T,
        gain_total[0],
    )


def fits(mesh):
    count = mesh.shape["seq"]
    return mesh.shape["book"] == 4 and count == 8


def solution(mesh):
    placed = (
        P("book", "seq", None),
        P("book", None),
        P("book", "seq", None),
        P(),
        P(None, ("seq", "book")),
        P(),
        P("book", "seq", None),
    )
    return jax.shard_map(
        per_device if fits(mesh) else per_device_gather,
        mesh=mesh,
        in_specs=placed,
        out_specs=(P("book", "seq", None), P(None, "book", None), P(None, ("seq", "book")), P()),
        check_vma=False,
    )
```

```python
import functools

import jax
import jax.numpy as jnp
from jax import lax
from jax.experimental import pallas as pl
from jax.experimental.pallas import tpu as pltpu
from jax.sharding import PartitionSpec as P

F32 = jnp.float32
BF16 = jnp.bfloat16
HEAVY = 8000000000
VMEM = pl.BlockSpec(memory_space=pltpu.VMEM)
SMEM = pl.BlockSpec(memory_space=pltpu.SMEM)


def shifted(block, axis, distance):
    devices = range(lax.axis_size(axis))
    route = [(i - distance, i) for i in devices if i - distance in devices]
    return lax.ppermute(block, axis, route)


def book_mask(position, book_lengths, offset):
    starts = jnp.cumsum(book_lengths) - book_lengths
    start_of = jnp.max(jnp.where(starts[None, :] <= position[:, None], starts[None, :], 0), axis=1)
    return position - offset >= start_of


def per_device_gather(features, lengths, owner, w_enc, w_in, gain, cotangent):
    feature_rows = features[0]
    frames, channels = feature_rows.shape
    tap_count, _, latent_width = w_enc.shape
    seq_count = lax.axis_size("seq")
    book_count = lax.axis_size("book")
    capacity = max(2, frames // seq_count + 1)
    first_frame = lax.axis_index("seq") * frames
    position = first_frame + jnp.arange(frames + tap_count - 1, dtype=jnp.int32)
    tap_masks = [book_mask(position, lengths[0], offset) for offset in range(tap_count)]
    feats_wide = feature_rows.astype(jnp.float32)
    activated = jax.nn.elu(feats_wide).astype(jnp.bfloat16)
    left_edge = shifted(activated[frames - (tap_count - 1) :], "seq", 1)
    padded = jnp.concatenate([left_edge, activated], axis=0)
    tap_inputs = []
    for offset in range(tap_count):
        begin = tap_count - 1 - offset
        window = padded[begin : begin + frames]
        tap_inputs.append(
            jnp.where(tap_masks[offset][:frames, None], window, jnp.zeros_like(window))
        )
    stacked = jnp.concatenate(tap_inputs, axis=1)
    latent = jnp.dot(
        stacked,
        w_enc.reshape(tap_count * channels, latent_width),
        preferred_element_type=jnp.float32,
    ).astype(jnp.bfloat16)
    owner_rank = owner[0, :, 0]
    one_hot = (owner_rank[:, None] == jnp.arange(seq_count, dtype=jnp.int32)[None, :]).astype(
        jnp.int32
    )
    slot_rank = jnp.sum((jnp.cumsum(one_hot, axis=0) - one_hot) * one_hot, axis=1)
    slot_index = owner_rank * capacity + slot_rank
    placement = (
        slot_index[:, None] == jnp.arange(seq_count * capacity, dtype=jnp.int32)[None, :]
    ).astype(jnp.bfloat16)
    outgoing = lax.dot_general(
        placement, latent, (((0,), (0,)), ((), ())), preferred_element_type=jnp.float32
    ).astype(jnp.bfloat16)
    arrived = lax.all_to_all(
        outgoing.reshape(seq_count, capacity, latent_width),
        "seq",
        split_axis=0,
        concat_axis=0,
        tiled=True,
    )
    arrived = arrived.reshape(seq_count * capacity, latent_width)
    w_full = lax.all_gather(w_in, ("seq", "book"), axis=1, tiled=True)
    grad_out = cotangent[0].astype(jnp.float32)
    hidden = jnp.dot(arrived, w_full, preferred_element_type=jnp.float32)
    inv_rms = lax.rsqrt(jnp.mean(hidden * hidden, axis=1, keepdims=True) + 1e-05)
    normed = hidden * inv_rms
    gain_term = grad_out * gain[None, :]
    hidden_grad = (
        inv_rms * (gain_term - normed * jnp.mean(gain_term * normed, axis=1, keepdims=True))
    ).astype(jnp.bfloat16)
    latent_back = lax.dot_general(
        hidden_grad, w_full, (((1,), (1,)), ((), ())), preferred_element_type=jnp.float32
    ).astype(jnp.bfloat16)
    w_part = lax.dot_general(
        arrived, hidden_grad, (((0,), (0,)), ((), ())), preferred_element_type=jnp.float32
    )
    gain_part = jnp.sum(grad_out * normed, axis=0)
    returned = lax.all_to_all(
        latent_back.reshape(seq_count, capacity, latent_width),
        "seq",
        split_axis=0,
        concat_axis=0,
        tiled=True,
    )
    returned = returned.reshape(seq_count * capacity, latent_width)
    latent_grad = jnp.dot(placement, returned, preferred_element_type=jnp.float32).astype(
        jnp.bfloat16
    )
    right_edge = shifted(latent_grad[: tap_count - 1], "seq", -1)
    extended = jnp.concatenate([latent_grad, right_edge], axis=0)
    tap_grads = []
    for offset in range(tap_count):
        window = extended[offset : offset + frames]
        tap_grads.append(
            jnp.where(
                tap_masks[offset][offset : offset + frames, None], window, jnp.zeros_like(window)
            )
        )
    kernel_back = jnp.transpose(w_enc, (0, 2, 1)).reshape(tap_count * latent_width, channels)
    activ_grad = jnp.dot(
        jnp.concatenate(tap_grads, axis=1), kernel_back, preferred_element_type=jnp.float32
    )
    slope = jnp.where(feats_wide > 0, 1.0, jnp.exp(feats_wide))
    feature_grad = (slope * activ_grad).astype(jnp.bfloat16)
    kernel_part = lax.dot_general(
        stacked, latent_grad, (((0,), (0,)), ((), ())), preferred_element_type=jnp.float32
    )
    kernel_part = kernel_part.reshape(tap_count, channels, latent_width)
    kernel_total, gain_total = lax.psum((kernel_part, gain_part), ("seq", "book"))
    share_width = channels // book_count
    kernel_mine = lax.dynamic_slice_in_dim(
        kernel_total, lax.axis_index("book") * share_width, share_width, 1
    )
    columns = w_in.shape[1]
    split_grad = w_part.reshape(latent_width, seq_count, book_count * columns)
    split_grad = lax.psum_scatter(
        split_grad.astype(jnp.bfloat16), "book", scatter_dimension=2, tiled=True
    ).astype(jnp.float32)
    w_grad = lax.psum_scatter(split_grad, "seq", scatter_dimension=1, tiled=True).reshape(
        latent_width, columns
    )
    return (feature_grad[None], kernel_mine, w_grad, gain_total)


def round_up(value, unit):
    return -(-value // unit) * unit


def swap(block, axis, mask):
    return lax.ppermute(block, axis, [(i, i ^ mask) for i in range(lax.axis_size(axis))])


def after(block, *others):
    return lax.optimization_barrier((block, *others))[0]


def iota(shape, dim):
    return lax.broadcasted_iota(jnp.int32, shape, dim)


def elu_wide(x):
    low = jnp.minimum(x, 0.0)
    series = 1.0 + low / 6.0
    for order in (5.0, 4.0, 3.0, 2.0):
        series = 1.0 + (low / order) * series
    below = jnp.where(low > -0.25, low * series, jnp.exp(low) - 1.0)
    return jnp.where(x > 0, x, below)


def start_below(position, lengths_ref):
    best = jnp.zeros_like(position)
    start = jnp.int32(0)
    for book in range(lengths_ref.shape[0]):
        best = jnp.where(start <= position, jnp.maximum(best, start), best)
        start = start + lengths_ref[book]
    return best


def ranks_of(owner_rows, seq_count):
    blocks, frames = owner_rows.shape
    parts = [
        (iota((seq_count, frames), 0) == owner_rows[b : b + 1].astype(jnp.int32)).astype(F32)
        for b in range(blocks)
    ]
    named = jnp.concatenate(parts, axis=0)
    before = (iota((frames, frames), 0) < iota((frames, frames), 1)).astype(BF16)
    counted = jnp.dot(named.astype(BF16), before, preferred_element_type=F32) * named
    return jnp.concatenate(
        [
            jnp.sum(counted[b * seq_count : (b + 1) * seq_count], axis=0, keepdims=True)
            for b in range(blocks)
        ],
        axis=0,
    )


def activate_kernel(feat_ref, padded_ref, turned_ref):
    frames, channels = feat_ref.shape
    act = elu_wide(feat_ref[...].astype(F32)).astype(BF16).astype(F32)
    padded_ref[0:8, :] = jnp.zeros((8, channels), F32)
    padded_ref[8 : 8 + frames, :] = act
    padded_ref[8 + frames :, :] = jnp.zeros((16, channels), F32)
    turned_ref[...] = act.T.astype(BF16)


def collect_kernel(plan, *refs):
    out_ref, at = refs[-1], 0
    for index, start, rows in plan:
        out_ref[at : at + rows, :] = refs[index][start : start + rows, :]
        at += rows


def encode_kernel(piece, lengths_ref, padded, owner_ref, w_ref, out_ref, extra):
    frames, latent_width = owner_ref.shape[1], out_ref.shape[1]
    taps = w_ref.shape[0]
    edges = taps - 1
    me = lax.axis_index("seq")
    seq_count = out_ref.shape[0] // piece
    owner = owner_ref[...]
    rank = ranks_of(owner, seq_count).astype(jnp.int32)
    row = jnp.bitwise_xor(owner, me) * piece + rank
    placed = (iota((seq_count * piece, frames), 0) == row).astype(F32).astype(BF16)
    position = me * frames + iota((frames, 1), 0)
    start_of = start_below(position, lengths_ref)
    beyond = (me + 1) * frames + iota((16, 1), 0)
    start_beyond = start_below(beyond, lengths_ref)
    total = jnp.zeros((frames, latent_width), F32)
    edge = jnp.zeros((16, latent_width), F32)
    for tap in range(taps):
        window = padded[8 - tap : 8 - tap + frames, :]
        window = jnp.where(position - tap >= start_of, window, 0.0).astype(BF16)
        total = total + jnp.dot(window, w_ref[tap], preferred_element_type=F32)
        if tap:
            window = padded[8 + frames - tap : 24 + frames - tap, :]
            window = jnp.where(beyond - tap >= start_beyond, window, 0.0).astype(BF16)
            edge = edge + jnp.dot(window, w_ref[tap], preferred_element_type=F32)
    latent = total.astype(BF16)
    outgoing = jnp.dot(placed, latent, preferred_element_type=F32)
    first, edge = total[:edges], edge[:edges]
    high = edge.astype(BF16).astype(F32)
    extra[...] = jnp.zeros_like(extra)
    at = piece - 1 - 3 * edges
    extra[at : at + edges, :] = first - latent[:8].astype(F32)[:edges]
    extra[at + edges : at + 2 * edges, :] = high
    extra[at + 2 * edges : at + 3 * edges, :] = edge - high
    extra[piece - 1 : piece, 0:frames] = owner.astype(F32)
    for rel in range(seq_count):
        here = slice(rel * piece, (rel + 1) * piece)
        out_ref[here, :] = (outgoing[here] + extra[...]).astype(BF16)


def join_rows_kernel(skip, *refs):
    rows = refs[0].shape[0] - skip
    for index, ref in enumerate(refs[:-1]):
        refs[-1][index * rows : (index + 1) * rows, :] = ref[skip:, :]


def middle_kernel(piece, capacity, frames, count, columns, edges, *refs):
    far_count = count // 2
    gathered, w_refs = refs[0], refs[1:9]
    gain_ref, cot_ref, back_ref, hg_ref, arrived_ref, owners_ref, w_full, hidden, back = refs[9:]
    slots, width = cot_ref.shape
    rows = back_ref.shape[0]
    latent_width = back_ref.shape[1]
    seq, book = lax.axis_index("seq"), lax.axis_index("book")
    for rel in range(count):
        line = gathered[rel * piece : (rel + 1) * piece, 0:frames].astype(F32)
        owners_ref[pl.ds(jnp.bitwise_xor(seq, rel), 1), :] = line[piece - 1 : piece, :]
    for index, w_ref in enumerate(w_refs):
        near_seq, near_y, near_core = index & 1, (index >> 1) & 1, index >> 2
        for far in range(far_count):
            at = jnp.bitwise_xor(seq, 2 * far + near_seq) * 4 + jnp.bitwise_xor(
                book, near_y * 2 + near_core
            )
            w_full[pl.ds(pl.multiple_of(at * columns, columns), columns), :] = w_ref[
                far * columns : (far + 1) * columns, :
            ]
    slot = iota((rows, 1), 0)
    source = jnp.zeros_like(slot)
    for block in range(1, count):
        source = source + (slot >= block * capacity).astype(jnp.int32)
    place = slot - source * capacity
    base = jnp.bitwise_xor(source, seq) * piece
    before = jnp.bitwise_xor(source - 1, seq) * piece
    column = iota((rows, count * piece), 1)
    picked = column == jnp.where(slot < slots, base + place, -1)
    taken = jnp.zeros_like(slot)
    at = piece - 1 - 3 * edges
    for edge in range(edges):
        owner = jnp.zeros((rows, 1), F32)
        for block in range(count):
            owner = jnp.where(source == block, owners_ref[block : block + 1, edge : edge + 1], owner)
        mine = (owner == seq.astype(F32)) & (slot < slots)
        here = mine & (place == taken)
        taken = taken + mine.astype(jnp.int32)
        rest = jnp.where(here, base + at + edge, -1)
        share = jnp.where(here & (source > 0), before + at + edges + edge, -1)
        share_rest = jnp.where(share >= 0, share + edges, -1)
        picked = picked | (column == rest) | (column == share) | (column == share_rest)
    picked = picked.astype(F32).astype(BF16)
    arrived = jnp.dot(picked, gathered[...], preferred_element_type=F32).astype(BF16)
    arrived_ref[...] = arrived
    step = latent_width
    squares = jnp.zeros((slots, step), F32)
    crossed = jnp.zeros((slots, step), F32)
    for at in range(0, width, step):
        part = lax.dot_general(
            arrived, w_full[at : at + step, :], (((1,), (1,)), ((), ())), preferred_element_type=F32
        )[:slots]
        hidden[:, at : at + step] = part
        squares = squares + part * part
        scaled = cot_ref[:, at : at + step].astype(F32) * gain_ref[:, at : at + step]
        crossed = crossed + part * scaled
    inv = lax.rsqrt(jnp.sum(squares, axis=1, keepdims=True) / width + 1e-05)
    pull = inv * inv * (jnp.sum(crossed, axis=1, keepdims=True) / width)
    total = jnp.zeros((rows, latent_width), F32)
    for at in range(0, width, step):
        part = hidden[:, at : at + step]
        grad_out = cot_ref[:, at : at + step].astype(F32)
        scaled = grad_out * gain_ref[:, at : at + step]
        grad = inv * (scaled - part * pull)
        grad = jnp.concatenate([grad, jnp.zeros((rows - slots, step), F32)], axis=0).astype(BF16)
        hg_ref[:, at : at + step] = grad
        total = total + jnp.dot(grad, w_full[at : at + step, :], preferred_element_type=F32)
        line = slots + at // step
        back[line : line + 1, :] = jnp.sum(grad_out * (part * inv), axis=0, keepdims=True)
    back[0:slots, :] = total[:slots]
    for line in range(slots + width // step, rows):
        back[line : line + 1, :] = jnp.zeros((1, latent_width), F32)
    back_ref[...] = back[...].astype(BF16)


def chip_order(count):
    return [(y, near, far) for y in (0, 1) for near in (0, 1) for far in range(count // 2)]


def projection_kernel(count, hg_ref, arrived_ref, send_ref, keep_ref):
    seq, book = lax.axis_index("seq"), lax.axis_index("book")
    core = jnp.bitwise_and(book, 1)
    chip = seq * 2 + (book >> 1)
    half = send_ref.shape[1]
    arrived = arrived_ref[...]
    for place, (y, near, far) in enumerate(chip_order(count)):
        at = jnp.bitwise_xor(chip, (2 * far + near) * 2 + y)
        grad = hg_ref[:, pl.ds(pl.multiple_of(at * 2 * half, 2 * half), 2 * half)]
        part = lax.dot_general(
            grad, arrived, (((0,), (0,)), ((), ())), preferred_element_type=F32
        )
        low, high = part[:half], part[half:]
        send_ref[place] = jnp.where(core == 0, high, low).astype(BF16)
        keep_ref[place] = jnp.where(core == 0, low, high).astype(BF16)


def prepare_kernel(capacity, rows, lengths_ref, owners_ref, facts_ref):
    count, frames = owners_ref.shape
    taps = facts_ref.shape[1]
    me = lax.axis_index("seq")
    owners = owners_ref[...]
    ranks = ranks_of(owners, count)
    position = iota((count, frames), 0) * frames + iota((count, frames), 1)
    relative = jnp.bitwise_xor(owners.astype(jnp.int32), me)
    relative = jnp.where(relative & 1 == 1, -count, relative >> 1)
    rows_of = [relative.astype(F32), ranks]
    for tap in range(1, taps):
        later = position + tap
        valid = (later < count * frames) & (position >= start_below(later, lengths_ref))
        rows_of.append(valid.astype(F32))
    eye = (iota((frames, frames), 0) == iota((frames, frames), 1)).astype(BF16)
    owner, rank, *valid = [
        lax.dot_general(
            eye, lines.astype(BF16), (((1,), (1,)), ((), ())), preferred_element_type=F32
        )
        for lines in rows_of
    ]
    lane = iota((frames, taps), 1)
    for block in range(count):
        here = slice(block, block + 1)
        facts = owner[:, here] * rows + (rank[:, here] + block * capacity)
        for tap in range(1, taps):
            facts = jnp.where(lane == tap, valid[tap - 1][:, here], facts)
        facts_ref[block * frames : (block + 1) * frames, :] = facts.astype(jnp.int32)


def spread_kernel(count, frames, taps, *refs):
    backs = refs[: count // 2]
    lines_ref, facts_ref, send_ref, windows_ref, gain_ref, own_ref, peer_ref = refs[count // 2 : -2]
    gathered, wide = refs[-2:]
    rows, latent_width = backs[0].shape
    share = lines_ref.shape[0] // 2
    gain_rows = gain_ref.shape[0]
    gain = jnp.zeros((gain_rows, latent_width), F32)
    for far, back_ref in enumerate(backs):
        gathered[far * rows : (far + 1) * rows, :] = back_ref[...]
        gain = gain + back_ref[...].astype(F32)[rows - gain_rows :]
    gain_ref[...] = gain
    for block in range(count):
        here = slice(block * frames, (block + 1) * frames)
        placed = iota((frames, gathered.shape[0]), 1) == facts_ref[here, 0:1]
        wide[here, :] = jnp.dot(
            placed.astype(F32).astype(BF16), gathered[...], preferred_element_type=F32
        )
    wide[count * frames :, :] = jnp.zeros((16, latent_width), F32)
    me = lax.axis_index("seq")
    for out_ref, block in ((own_ref, me), (peer_ref, jnp.bitwise_xor(me, 1))):
        at = pl.multiple_of(block * frames, frames)
        out_ref[...] = wide[pl.ds(at, frames + 16), :].astype(BF16)
    for block in range(count):
        here = slice(block * frames, (block + 1) * frames)
        windows_ref[here, 0:latent_width] = wide[here, :].astype(BF16)
        for tap in range(1, taps):
            later = wide[block * frames + tap : (block + 1) * frames + tap, :]
            later = jnp.where(facts_ref[here, tap : tap + 1] > 0, later, 0.0)
            windows_ref[here, tap * latent_width : (tap + 1) * latent_width] = later.astype(BF16)
    part = jnp.dot(lines_ref[...], windows_ref[...], preferred_element_type=F32)
    for y in (0, 1):
        for tap in range(taps):
            at = (y * taps + tap) * share
            send_ref[at : at + share, :] = part[
                y * share : (y + 1) * share, tap * latent_width : (tap + 1) * latent_width
            ].astype(BF16)
    high = gain.astype(BF16)
    at = 2 * taps * share
    send_ref[at : at + 2 * gain_rows, :] = jnp.concatenate(
        [high.astype(F32), gain - high.astype(F32)], axis=0
    ).astype(BF16)


def channel_kernel(orders, *refs):
    turned_refs, out_refs = refs[: len(orders)], refs[len(orders) :]
    seq, book = lax.axis_index("seq"), lax.axis_index("book")
    share = turned_refs[0].shape[1] // 4
    for turned_ref, order in zip(turned_refs, orders):
        frames = turned_ref.shape[2]
        for index, rel in enumerate(order):
            lanes = pl.ds(pl.multiple_of(jnp.bitwise_xor(seq, rel) * frames, frames), frames)
            for core, out_ref in enumerate(out_refs):
                for y in (0, 1):
                    at = jnp.bitwise_xor(book, 2 * y + core) * share
                    out_ref[y * share : (y + 1) * share, lanes] = turned_ref[
                        index, pl.ds(pl.multiple_of(at, share), share), :
                    ]


def own_part_kernel(taps, lines_ref, windows_ref, out_ref):
    share, latent_width = lines_ref.shape[0] // 2, out_ref.shape[1]
    part = jnp.dot(lines_ref[...], windows_ref[...], preferred_element_type=F32)
    for y in (0, 1):
        for tap in range(taps):
            at = (y * taps + tap) * share
            out_ref[at : at + share, :] = part[
                y * share : (y + 1) * share, tap * latent_width : (tap + 1) * latent_width
            ]


def fold_kernel(kept_ref, got_ref, gain_ref, send_ref, mine_ref, gain_out_ref):
    half, gain_rows = mine_ref.shape[0], gain_ref.shape[0]
    mine_ref[...] = kept_ref[0:half, :] + got_ref[0:half, :].astype(F32)
    send_ref[0:half, :] = (
        kept_ref[half : 2 * half, :] + got_ref[half : 2 * half, :].astype(F32)
    ).astype(BF16)
    pair = got_ref[2 * half : 2 * half + 2 * gain_rows, :].astype(F32)
    gain = gain_ref[...] + (pair[:gain_rows] + pair[gain_rows:])
    gain_out_ref[...] = gain
    high = gain.astype(BF16).astype(F32)
    send_ref[half : half + 2 * gain_rows, :] = jnp.concatenate(
        [high, gain - high], axis=0
    ).astype(BF16)


def sum_kernel(mine_ref, got_ref, gain_ref, send_ref):
    half, gain_rows = mine_ref.shape[0], gain_ref.shape[0]
    send_ref[0:half, :] = (mine_ref[...] + got_ref[0:half, :].astype(F32)).astype(BF16)
    pair = got_ref[half : half + 2 * gain_rows, :].astype(F32)
    gain = gain_ref[...] + (pair[:gain_rows] + pair[gain_rows:])
    high = gain.astype(BF16).astype(F32)
    send_ref[half : half + 2 * gain_rows, :] = jnp.concatenate(
        [high, gain - high], axis=0
    ).astype(BF16)


def finish_kernel(mine_ref, got_ref, out_ref, gain_out_ref):
    half = out_ref.shape[0]
    gain_rows = (mine_ref.shape[0] - half) // 2
    out_ref[...] = mine_ref[0:half, :].astype(F32) + got_ref[0:half, :].astype(F32)
    gain = jnp.zeros((gain_rows, mine_ref.shape[1]), F32)
    for ref in (mine_ref, got_ref):
        pair = ref[half : half + 2 * gain_rows, :].astype(F32)
        gain = gain + (pair[:gain_rows] + pair[gain_rows:])
    step = gain.shape[1]
    for line in range(gain_rows):
        gain_out_ref[:, line * step : (line + 1) * step] = gain[line : line + 1]


def feature_kernel(feat_ref, own_ref, got_ref, facts_ref, w_ref, out_ref, wide):
    frames = feat_ref.shape[0]
    at = pl.multiple_of(lax.axis_index("seq") * frames, frames)
    wide[...] = own_ref[...].astype(F32) + got_ref[...].astype(F32)
    facts = facts_ref[pl.ds(at, frames), :]
    total = jnp.zeros(feat_ref.shape, F32)
    for tap in range(w_ref.shape[0]):
        window = wide[tap : tap + frames, :]
        if tap:
            window = jnp.where(facts[:, tap : tap + 1] > 0, window, 0.0)
        total = total + lax.dot_general(
            window.astype(BF16), w_ref[tap], (((1,), (1,)), ((), ())), preferred_element_type=F32
        )
    feats = feat_ref[...].astype(F32)
    slope = jnp.where(feats > 0, 1.0, jnp.exp(jnp.minimum(feats, 0.0)))
    out_ref[...] = (slope * total).astype(BF16)


def call(kernel, outs, operands, scratch=(), smem=0, flops=0):
    return pl.pallas_call(
        kernel,
        out_shape=outs,
        in_specs=[SMEM] * smem + [VMEM] * (len(operands) - smem),
        out_specs=jax.tree.map(lambda _: VMEM, outs),
        scratch_shapes=list(scratch),
        compiler_params=pltpu.CompilerParams(vmem_limit_bytes=24 * 2**20),
        cost_estimate=pl.CostEstimate(flops=flops, bytes_accessed=1024, transcendentals=0),
    )(*operands)


def collect(blocks, flops=0):
    arrays, plan = [], []
    for array, start, rows in blocks:
        found = [i for i, known in enumerate(arrays) if known is array]
        if not found:
            arrays.append(array)
        plan.append((found[0] if found else len(arrays) - 1, start, rows))
    total = sum(rows for _, _, rows in plan)
    (out,) = call(
        functools.partial(collect_kernel, tuple(plan)),
        [shape((total, arrays[0].shape[1]), arrays[0].dtype)],
        tuple(arrays),
        flops=flops,
    )
    return out


def shape(dims, dtype=BF16):
    return jax.ShapeDtypeStruct(dims, dtype)


def per_device(features, lengths, owner, w_enc, w_in, gain, cotangent):
    feats = features[0]
    cot = cotangent[0]
    book_lengths = lengths[0]
    frames, channels = feats.shape
    taps, _, latent_width = w_enc.shape
    slots, width = cot.shape
    count = lax.axis_size("seq")
    far_count = count // 2
    fars = range(1, far_count)
    capacity = max(2, frames // count + 1)
    piece = round_up(capacity + 1 + 3 * (taps - 1), 16)
    gain_rows = width // latent_width
    rows = round_up(slots + gain_rows, 16)
    half = channels // 4

    columns = w_in.shape[1]
    padded, turned = call(
        activate_kernel,
        [shape((24 + frames, channels), F32), shape((channels, frames))],
        (feats,),
        flops=HEAVY // 10,
    )
    (sent,) = call(
        functools.partial(encode_kernel, piece),
        [shape((count * piece, latent_width))],
        (book_lengths, padded, owner[0].T, w_enc),
        scratch=[pltpu.VMEM((piece, latent_width), F32)],
        smem=1,
    )
    pieces = {0: {far: (sent, 2 * far * piece, 2 * piece) for far in range(far_count)}}
    w_blocks = {0: (w_in.T, 0, columns)}
    held, mask = turned[None], far_count // 2
    w_got = None
    while mask:
        sources = sorted(pieces)
        owners = [far for far in range(far_count) if far in pieces[0] and far & mask]
        message = [w_blocks[far] for far in sources]
        message += [pieces[source][far] for source in sources for far in owners]
        w_got = swap(collect(message), "seq", 2 * mask)
        at = 0
        for source in sources:
            w_blocks[source ^ mask] = (w_got, at, columns)
            at += columns
        for source in sources:
            pieces[source ^ mask] = {}
            for far in owners:
                pieces[source ^ mask][far ^ mask] = (w_got, at, 2 * piece)
                at += 2 * piece
                del pieces[source][far]
        if mask == far_count // 2:
            joined = collect([w_blocks[far] for far in sorted(w_blocks)], flops=HEAVY)
            w_blocks = {far: (joined, i * columns, columns) for i, far in enumerate(sorted(w_blocks))}
        if mask < far_count // 2:
            held = after(held, w_got)
        got = swap(held, "seq", 2 * mask)
        if mask == far_count // 2:
            held = jnp.concatenate([held, got])
        mask //= 2
    x_first, x_last = swap(held, "seq", 1), swap(got, "seq", 1)
    fars_of_w = [w_blocks[far] for far in range(far_count)]
    near = [pieces[far][0] for far in range(far_count)]
    x_send = collect(fars_of_w + [(array, at + piece, piece) for array, at, _ in near])
    w_line = collect(fars_of_w)
    x_got = swap(x_send, "seq", 1)
    w_side = swap(w_line, "book", 2)
    w_diag = swap(w_line, ("seq", "book"), 4 + 2)
    w_chips = [w_line, x_got, w_side, w_diag]
    turned_all = [held, got, x_first, x_last]
    orders = [[0, 4], [2, 6], [1, 5], [3, 7]]
    gathered = []
    for far, (array, at, _) in enumerate(near):
        gathered += [(array, at, piece), (x_got, far_count * columns + far * piece, piece)]
    gathered = collect(gathered, flops=HEAVY)
    w_pieces = w_chips + [
        swap(after(block, gathered) if block is x_got else block, "book", 1) for block in w_chips
    ]

    back, hidden_grad, arrived, owners = call(
        functools.partial(middle_kernel, piece, capacity, frames, count, columns, taps - 1),
        [
            shape((rows, latent_width)),
            shape((rows, width)),
            shape((rows, latent_width)),
            shape((count, frames), F32),
        ],
        (gathered, *w_pieces, gain[None], cot),
        scratch=[
            pltpu.VMEM((width, latent_width), BF16),
            pltpu.VMEM((slots, width), F32),
            pltpu.VMEM((rows, latent_width), F32),
        ],
        flops=HEAVY,
    )
    backs = [back] + [swap(back, "seq", 2 * far) for far in fars]
    (facts,) = call(
        functools.partial(prepare_kernel, capacity, rows),
        [shape((count * frames, taps), jnp.int32)],
        (book_lengths, owners),
        smem=1,
        flops=HEAVY,
    )
    w_send, w_keep = call(
        functools.partial(projection_kernel, count),
        [shape((2 * count, columns, latent_width))] * 2,
        (hidden_grad, arrived),
    )
    w_got, facts = lax.optimization_barrier((swap(w_send, "book", 1), facts))
    w_sum = w_keep.astype(F32) + w_got.astype(F32)
    w_parts = [w_sum[at : at + far_count].astype(BF16) for at in range(0, 2 * count, far_count)]
    w_x = swap(w_parts[1], "seq", 1)
    w_y = swap(w_parts[2], "book", 2)
    w_d = swap(w_parts[3], ("seq", "book"), 4 + 2)
    own_lines, sent_lines = call(
        functools.partial(channel_kernel, orders),
        [shape((2 * half, count * frames))] * 2,
        tuple(after(turned_all, *w_parts)),
        flops=HEAVY,
    )
    message = 2 * taps * half + 2 * gain_rows
    k_send, windows, gain_seq, lines_own, lines_peer = call(
        functools.partial(spread_kernel, count, frames, taps),
        [
            shape((message, latent_width)),
            shape((count * frames, taps * latent_width)),
            shape((gain_rows, latent_width), F32),
            shape((frames + 16, latent_width)),
            shape((frames + 16, latent_width)),
        ],
        (*backs, sent_lines, facts),
        scratch=[
            pltpu.VMEM((far_count * rows, latent_width), BF16),
            pltpu.VMEM((count * frames + 16, latent_width), F32),
        ],
        flops=HEAVY,
    )
    k_got = swap(k_send, "book", 1)
    (k_kept,) = call(
        functools.partial(own_part_kernel, taps),
        [shape((2 * taps * half, latent_width), F32)],
        (own_lines, windows),
        flops=HEAVY,
    )
    y_send, k_mine, gain_pair = call(
        fold_kernel,
        [
            shape((taps * half + 2 * gain_rows, latent_width)),
            shape((taps * half, latent_width), F32),
            shape((gain_rows, latent_width), F32),
        ],
        (k_kept, k_got, gain_seq),
    )
    y_got = swap(y_send, "book", 2)
    lines_got = swap(after(lines_peer, y_send), "seq", 1)
    w_x, w_y, w_d = after((w_x, w_y, w_d), y_send)
    w_sum = w_sum[:far_count] + w_x.astype(F32) + w_y.astype(F32) + w_d.astype(F32)
    w_far = [w_sum[far].astype(BF16) for far in fars]
    w_total = w_sum[0]
    w_got = [swap(block, "seq", 2 * far) for far, block in zip(fars, w_far)]
    (x_send,) = call(
        sum_kernel,
        [shape((taps * half + 2 * gain_rows, latent_width))],
        (k_mine, y_got, gain_pair),
    )
    x_got = swap(x_send, "seq", 1)
    (feature_grad,) = call(
        feature_kernel,
        [shape(feats.shape)],
        (feats, lines_own, lines_got, facts, w_enc),
        scratch=[pltpu.VMEM((frames + 16, latent_width), F32)],
        flops=HEAVY,
    )
    x_got = after(x_got, feature_grad)
    kernel_mine, gain_total = call(
        finish_kernel,
        [shape((taps * half, latent_width), F32), shape((1, width), F32)],
        (x_send, x_got),
    )
    for block in after(w_got, x_send):
        w_total = w_total + block.astype(F32)
    return (
        feature_grad[None],
        kernel_mine.reshape(taps, half, latent_width),
        w_total.T,
        gain_total[0],
    )


def fits(mesh):
    count = mesh.shape["seq"]
    return mesh.shape["book"] == 4 and count == 8


def solution(mesh):
    placed = (
        P("book", "seq", None),
        P("book", None),
        P("book", "seq", None),
        P(),
        P(None, ("seq", "book")),
        P(),
        P("book", "seq", None),
    )
    return jax.shard_map(
        per_device if fits(mesh) else per_device_gather,
        mesh=mesh,
        in_specs=placed,
        out_specs=(P("book", "seq", None), P(None, "book", None), P(None, ("seq", "book")), P()),
        check_vma=False,
    )
```
